512 devices in a mesh: section: 16 (over y_lo, z), expert: 32 (over x, y_hi, core).
Axes of the slice: x: 4, y: 8 (y_hi: 4, y_lo: 2; y = y_hi * 2 + y_lo), z: 8, core: 2. Of those that a mesh axis runs over, the one named last changes fastest.
Arguments:
- act_fwd: bfloat16 [16, 256, 3584], P('section', 'expert'), may hold values from -6 to 6
- route_fwd: int32 [16, 256, 2], P('section', 'expert'), may hold values from 0 to 3, as said below
- slot_fwd: int32 [16, 256, 2], P('section', 'expert'), may hold values from 0 to 7, as said below
- weight_fwd: float32 [16, 256, 2], P('section', 'expert'), may hold values from 0.1 to 1
- grad_bwd: bfloat16 [16, 256, 3584], P('section', 'expert'), may hold values from -6 to 6
- route_bwd: int32 [16, 256, 2], P('section', 'expert'), may hold values from 0 to 3, as said below
- slot_bwd: int32 [16, 256, 2], P('section', 'expert'), may hold values from 0 to 7, as said below
- weight_bwd: float32 [16, 256, 2], P('section', 'expert'), may hold values from 0.1 to 1
- saved_gate: bfloat16 [16, 32, 8, 4096], P('section', None, None, 'expert'), may hold values from -6 to 6
- saved_up: bfloat16 [16, 32, 8, 4096], P('section', None, None, 'expert'), may hold values from -6 to 6
- w_gate: bfloat16 [16, 3584, 4096], P('section', None, 'expert'), may hold values from -0.09375 to 0.09375
- w_up: bfloat16 [16, 3584, 4096], P('section', None, 'expert'), may hold values from -0.09375 to 0.09375
- w_down: bfloat16 [16, 4096, 3584], P('section', 'expert'), may hold values from -0.1875 to 0.1875
Outputs:
- fwd_next: bfloat16 [16, 256, 3584], P('section', 'expert')
- bwd_prev: bfloat16 [16, 256, 3584], P('section', 'expert')
The draws below stay inside these ranges and needn't reach their ends.
Inputs may be any that keep to these rules, and one draw needn't show every extreme that they name: `route_fwd`: each token names 2 different experts. Within the 8 tokens of one block, no expert is named more than 8 times, and one expert is named exactly 8 times. `slot_fwd`: within one block, the tokens naming one expert hold distinct slots 0 to their count - 1. `route_bwd`: as for route_fwd. `slot_bwd`: as for slot_fwd, with route_bwd.
All inputs are finite; a program needn't handle non-finite values.
Results may differ from the reference program's by a relative error of at most 0.005.
Values may be sent and summed in bfloat16 or wider, within the bound.
A program may use at most 64 MiB of HBM per device.

```python
import math
import jax
import jax.numpy as jnp
from jax import lax

D = 3584
HID = 1024
EXP_WIN = 4
TOPK = 2
TOK_DEV = 8
CAP = 8
HID_TOT = 4096
TOKENS = 256
N_SECTION = 16
N_EXPERT = 32


def routing_table(key):
    blocks = N_SECTION * N_EXPERT
    key_hot, key_other, key_side, key_order = jax.random.split(key, 4)
    hot_expert = jax.random.randint(key_hot, (blocks, 1), 0, EXP_WIN)
    offset_draw = jax.random.randint(key_other, (blocks, TOK_DEV), 1, EXP_WIN)
    other_expert = (hot_expert + offset_draw) % EXP_WIN
    side_bit = jax.random.randint(key_side, (blocks, TOK_DEV), 0, 2)
    first_pick = jnp.where(side_bit == 1, hot_expert, other_expert)
    second_pick = jnp.where(side_bit == 1, other_expert, hot_expert)
    chosen = jnp.stack([first_pick, second_pick], axis=-1)
    priority = jax.random.randint(key_order, (blocks, TOK_DEV), 0, 1024) * TOK_DEV + jnp.arange(TOK_DEV)[None, :]
    named_by = jnp.any(chosen[:, :, :, None] == jnp.arange(EXP_WIN)[None, None, None, :], axis=2)
    earlier = priority[:, None, :] < priority[:, :, None]
    slot_each = jnp.sum((earlier[:, :, :, None] & named_by[:, None, :, :]).astype(jnp.int32), axis=2)
    match_pick = chosen[:, :, :, None] == jnp.arange(EXP_WIN)[None, None, None, :]
    slot_pick = jnp.sum(jnp.where(match_pick, slot_each[:, :, None, :], 0), axis=-1)
    route_out = chosen.reshape(N_SECTION, N_EXPERT * TOK_DEV, TOPK).astype(jnp.int32)
    slot_out = slot_pick.reshape(N_SECTION, N_EXPERT * TOK_DEV, TOPK).astype(jnp.int32)
    return (route_out, slot_out)


def draw_route_fwd(key, part):
    return routing_table(jax.random.fold_in(key, 11))[0]


def draw_slot_fwd(key, part):
    return routing_table(jax.random.fold_in(key, 11))[1]


def draw_route_bwd(key, part):
    return routing_table(jax.random.fold_in(key, 12))[0]


def draw_slot_bwd(key, part):
    return routing_table(jax.random.fold_in(key, 12))[1]


def steps_of(rng, extent, cuts, smallest, high):
    level = 1.0
    for dim, parts in cuts:
        draws = jax.random.uniform(jax.random.fold_in(jax.random.fold_in(rng, 6), dim), (parts,), jnp.float32, smallest / len(cuts), high / len(cuts))
        level = level * jnp.repeat(jnp.exp(draws), extent[dim] // parts).reshape((-1,) + (1,) * (len(extent) - 1 - dim))
    return level


def scatter_about(stream_key, dims, spread, reach, cuts=(), held_as=jnp.bfloat16):
    drawn = spread * jax.random.normal(stream_key, dims, jnp.float32)
    if cuts:
        drawn = drawn * steps_of(stream_key, dims, cuts, -0.22, 0.18)
    return jnp.clip(drawn, -reach, reach).astype(held_as)


def setup_inputs(seed: int = 0) -> dict:
    splits = jax.random.split(jax.random.key(seed), 14)
    return {
        "act_fwd": scatter_about(splits[0], (N_SECTION, TOKENS, D), 1.0, 6.0, ((0, 16), (1, 32))),
        "route_fwd": draw_route_fwd(jax.random.fold_in(splits[13], 71), 0),
        "slot_fwd": draw_slot_fwd(jax.random.fold_in(splits[13], 71), 0),
        "weight_fwd": jnp.clip(jnp.exp(math.log(1.0) - 2.3025851 * jax.random.uniform(splits[3], (N_SECTION, TOKENS, TOPK), jnp.float32) ** steps_of(splits[3], (N_SECTION, TOKENS, TOPK), ((0, 16), (1, 32)), -0.2, 0.2)), 0.1, 1.0),
        "grad_bwd": scatter_about(splits[4], (N_SECTION, TOKENS, D), 1.0, 6.0, ((0, 16), (1, 32))),
        "route_bwd": draw_route_bwd(jax.random.fold_in(splits[13], 71), 0),
        "slot_bwd": draw_slot_bwd(jax.random.fold_in(splits[13], 71), 0),
        "weight_bwd": jnp.clip(jnp.exp(math.log(1.0) - 2.3025851 * jax.random.uniform(splits[7], (N_SECTION, TOKENS, TOPK), jnp.float32) ** steps_of(splits[7], (N_SECTION, TOKENS, TOPK), ((0, 16), (1, 32)), -0.2, 0.2)), 0.1, 1.0),
        "saved_gate": scatter_about(splits[8], (N_SECTION, N_EXPERT, CAP, HID_TOT), 1.0, 6.0, ((0, 16), (3, 32))),
        "saved_up": scatter_about(splits[9], (N_SECTION, N_EXPERT, CAP, HID_TOT), 1.0, 6.0, ((0, 16), (3, 32))),
        "w_gate": scatter_about(splits[10], (N_SECTION, D, HID_TOT), D ** -0.5, 0.09375, ((0, 16), (2, 32))),
        "w_up": scatter_about(splits[11], (N_SECTION, D, HID_TOT), D ** -0.5, 0.09375, ((0, 16), (2, 32))),
        "w_down": scatter_about(splits[12], (N_SECTION, HID_TOT, D), HID ** -0.5, 0.1875, ((0, 16), (1, 32))),
    }


def build_rows(tokens, route, slot, expert):
    blocks = tokens.reshape(N_EXPERT, TOK_DEV, D)
    route_b = route.reshape(N_EXPERT, TOK_DEV, TOPK, 1)
    slot_b = slot.reshape(N_EXPERT, TOK_DEV, TOPK, 1)
    matched = (route_b == expert) & (slot_b == jnp.arange(CAP, dtype=jnp.int32))
    taken = jnp.any(matched, axis=2)
    position = jnp.sum(taken.astype(jnp.int32) * jnp.arange(TOK_DEV, dtype=jnp.int32)[None, :, None], axis=1)
    filled = jnp.any(taken, axis=1)
    picked = jnp.take_along_axis(blocks, position[:, :, None].astype(jnp.int32), axis=1)
    picked = jnp.where(filled[:, :, None], picked, jnp.zeros_like(picked))
    return picked.reshape(N_EXPERT * CAP, D)


def rounded_sum(pieces):
    total = jnp.zeros(pieces[0].shape, jnp.float32)
    for piece in pieces:
        total = total + lax.optimization_barrier(piece.astype(jnp.bfloat16)).astype(jnp.float32)
    return total


def forward_expert(picked, gate_cols, up_cols, down_rows):
    group = N_EXPERT // EXP_WIN
    width = HID // group
    gate_val = jnp.dot(picked, gate_cols, preferred_element_type=jnp.float32)
    up_val = jnp.dot(picked, up_cols, preferred_element_type=jnp.float32)
    hidden = (jax.nn.silu(gate_val) * up_val).astype(jnp.bfloat16)
    pieces = []
    for member in range(group):
        lower = member * width
        pieces.append(jnp.dot(hidden[:, lower:lower + width], down_rows[lower:lower + width], preferred_element_type=jnp.float32))
    return rounded_sum(pieces)


def backward_expert(picked, gate_saved, up_saved, gate_cols, up_cols, down_rows):
    group = N_EXPERT // EXP_WIN
    width = HID // group
    grad_hidden = jnp.dot(picked, down_rows.T, preferred_element_type=jnp.float32)
    gate_val = gate_saved.astype(jnp.float32)
    up_val = up_saved.astype(jnp.float32)
    sigma = jax.nn.sigmoid(gate_val)
    slope = sigma * (1.0 + gate_val * (1.0 - sigma))
    grad_gate = (grad_hidden * up_val * slope).astype(jnp.bfloat16)
    grad_up = (grad_hidden * gate_val * sigma).astype(jnp.bfloat16)
    pieces = []
    for member in range(group):
        lower = member * width
        term = jnp.dot(grad_gate[:, lower:lower + width], gate_cols[:, lower:lower + width].T, preferred_element_type=jnp.float32)
        term = term + jnp.dot(grad_up[:, lower:lower + width], up_cols[:, lower:lower + width].T, preferred_element_type=jnp.float32)
        pieces.append(term)
    return rounded_sum(pieces)


def combine(base, outputs, route, slot, weight):
    flat = outputs.reshape(EXP_WIN * N_EXPERT * CAP, D)
    owner = (jnp.arange(TOKENS, dtype=jnp.int32) // TOK_DEV)[:, None]
    location = (route * (N_EXPERT * CAP) + owner * CAP + slot).astype(jnp.int32)
    gathered = flat[location]
    return (base.astype(jnp.float32) + jnp.sum(weight[:, :, None] * gathered, axis=1)).astype(jnp.bfloat16)


def reference(act_fwd, route_fwd, slot_fwd, weight_fwd, grad_bwd, route_bwd, slot_bwd, weight_bwd, saved_gate, saved_up, w_gate, w_up, w_down):
    forward_all = []
    backward_all = []
    for section in range(N_SECTION):
        outputs = []
        grads = []
        for expert in range(EXP_WIN):
            lower = expert * HID
            gate_cols = w_gate[section][:, lower:lower + HID]
            up_cols = w_up[section][:, lower:lower + HID]
            down_rows = w_down[section][lower:lower + HID]
            picked = build_rows(act_fwd[section], route_fwd[section], slot_fwd[section], expert)
            outputs.append(forward_expert(picked, gate_cols, up_cols, down_rows))
            picked_grad = build_rows(grad_bwd[section], route_bwd[section], slot_bwd[section], expert)
            gate_saved = saved_gate[section][:, :, lower:lower + HID].reshape(N_EXPERT * CAP, HID)
            up_saved = saved_up[section][:, :, lower:lower + HID].reshape(N_EXPERT * CAP, HID)
            grads.append(backward_expert(picked_grad, gate_saved, up_saved, gate_cols, up_cols, down_rows))
        forward_all.append(combine(act_fwd[section], jnp.stack(outputs), route_fwd[section], slot_fwd[section], weight_fwd[section]))
        backward_all.append(combine(grad_bwd[section], jnp.stack(grads), route_bwd[section], slot_bwd[section], weight_bwd[section]))
    fwd_next = jnp.roll(jnp.stack(forward_all), 1, axis=0)
    bwd_prev = jnp.roll(jnp.stack(backward_all), -1, axis=0)
    return fwd_next, bwd_prev
```

```python
import jax
import jax.numpy as jnp
from jax import lax
from jax.experimental import pallas as pl
from jax.experimental.pallas import tpu as pltpu
from jax.sharding import PartitionSpec as P

NX, NY, ROWS, D, HID = 4, 4, 8, 3584, 128
META = 128
HALF = D // 2
NC = 2
C = D // NC
KSTEP = 512
SUB = 256
BF, F32 = jnp.bfloat16, jnp.float32

Y_MINUS, Y_PLUS, Y_FAR_A, Y_FAR_B, X_MINUS, X_PLUS, X_FAR, SIB = 0, 1, 2, 3, 4, 8, 12, 16
N_GATHER = 20
C_SIB, C_FAR_P, C_FAR_M, C_ONE_P, C_ONE_M, C_TWO_P, C_TWO_M, C_YFAR, C_Y_P, C_Y_M, C_OWN = range(11)
N_COMBINE = 11


def dot(a, b):
    return lax.dot_general(a, b, (((1,), (0,)), ((), ())), preferred_element_type=F32)


def dot_t(a, b):
    return lax.dot_general(a, b, (((1,), (1,)), ((), ())), preferred_element_type=F32)


def routing_lanes(route, slot, weight, first):
    lane = lax.broadcasted_iota(jnp.int32, (ROWS, META), 1) - first
    square = (ROWS, ROWS)
    same = lax.broadcasted_iota(jnp.int32, square, 0) == lax.broadcasted_iota(jnp.int32, square, 1)

    def column(values, k):
        return jnp.sum(jnp.where(same, values[k : k + 1, :].astype(F32), 0.0), axis=1, keepdims=True)

    total = jnp.zeros((ROWS, META), F32)
    for k in range(2):
        expert = column(route, k).astype(jnp.int32)
        w = column(weight, k)
        hi = w.astype(BF).astype(F32)
        mid = (w - hi).astype(BF).astype(F32)
        low = w - hi - mid
        place = column(slot, k) + 1.0
        for i, part in enumerate((hi, mid, low, place)):
            total = total + jnp.where(lane == expert + 4 * i, part, 0.0)
    return total


def kernel(
    act, route_f, slot_f, weight_f, grad, route_b, slot_b, weight_b, saved_gate, saved_up, w_gate, w_up, w_down,
    out_f, out_b,
    xf, xb, wcat, wd, saved, ri, wi,
    part_f, part_b, sib_s, sib_r, far_s, far_r, near_s, near_r, yfar_s, yfar_r, ynear_s, ynear_r, own_s, own_r, base_r,
    gs, gr, cs, cr, bs, br, ls,
):
    sec = lax.axis_index("section")
    ex = lax.axis_index("expert")
    nsec = lax.axis_size("section")
    x, y, c = ex // (NY * 2), (ex // 2) % NY, ex % 2
    oc = 1 - c
    xs = [(x + i) % NX for i in range(NX)]
    ys = [(y + i) % NY for i in range(NY)]
    to = [(sec + 1) % nsec, (sec + nsec - 1) % nsec]

    def dev(xi, yi, ci, s=sec):
        return (s, xi * (NY * 2) + yi * 2 + ci)

    def copy(src, dst, send, recv, device):
        return pltpu.make_async_remote_copy(
            src_ref=src, dst_ref=dst, send_sem=send, recv_sem=recv, device_id=device,
            device_id_type=pl.DeviceIdType.MESH,
        )

    sib = dev(x, y, oc)
    x_to = {1: dev(xs[1], y, c), -1: dev(xs[3], y, c)}
    y_to = {1: dev(x, ys[1], c), -1: dev(x, ys[3], c)}
    gathered = (xf, xb)
    widths = (D + META, D)
    parts = (part_f, part_b)
    outs = (out_f, out_b)

    loads = [
        pltpu.make_async_copy(act.at[0], xf.at[x, y, c, :, pl.ds(0, D)], ls.at[0]),
        pltpu.make_async_copy(grad.at[0], xb.at[x, y, c], ls.at[1]),
        pltpu.make_async_copy(route_f.at[0], ri.at[0], ls.at[2]),
        pltpu.make_async_copy(slot_f.at[0], ri.at[1], ls.at[3]),
        pltpu.make_async_copy(route_b.at[0], ri.at[2], ls.at[4]),
        pltpu.make_async_copy(slot_b.at[0], ri.at[3], ls.at[5]),
        pltpu.make_async_copy(weight_f.at[0], wi.at[0], ls.at[6]),
        pltpu.make_async_copy(weight_b.at[0], wi.at[1], ls.at[7]),
        pltpu.make_async_copy(w_gate.at[0], wcat.at[:, pl.ds(0, HID)], ls.at[8]),
        pltpu.make_async_copy(w_up.at[0], wcat.at[:, pl.ds(HID, HID)], ls.at[9]),
        pltpu.make_async_copy(w_down.at[0], wd, ls.at[10]),
        pltpu.make_async_copy(saved_gate.at[0], saved.at[:, :, pl.ds(0, HID)], ls.at[11]),
        pltpu.make_async_copy(saved_up.at[0], saved.at[:, :, pl.ds(HID, HID)], ls.at[12]),
    ]
    for load in loads:
        load.start()

    barrier = pltpu.get_barrier_semaphore()
    partners = [sib, x_to[1], x_to[-1], y_to[1], y_to[-1]]
    partners += [dev(x, yi, c, s) for s in to for yi in (ys[0], ys[1], ys[3])]
    for partner in partners:
        pl.semaphore_signal(barrier, inc=1, device_id=partner, device_id_type=pl.DeviceIdType.MESH)
    for load in loads[2:8]:
        load.wait()
    lanes = routing_lanes(ri[0], ri[1], wi[0], 0) + routing_lanes(ri[2], ri[3], wi[1], 16)
    for load in loads[0:2]:
        load.wait()
    xf[x, y, c, :, pl.ds(D, META)] = lanes.astype(BF)
    pl.semaphore_wait(barrier, len(partners))

    def g_copy(p, ref, sem, device):
        return copy(ref, ref, gs.at[p, sem], gr.at[p, sem], device)

    def block(p, xi, yi):
        return gathered[p].at[xi, yi, c]

    def y_half(p, yi, half):
        cols = pl.ds(0, HALF) if half == 0 else pl.ds(HALF, widths[p] - HALF)
        return gathered[p].at[x, yi, c, :, cols]

    def sib_line(p, i):
        return g_copy(p, gathered[p].at[xs[i], :, c], SIB + i, sib)

    def send_x(p, r):
        g_copy(p, block(p, x, ys[r]), X_MINUS + r, x_to[1]).start()
        g_copy(p, block(p, x, ys[r]), X_PLUS + r, x_to[-1]).start()

    def x_in(p, r):
        g_copy(p, block(p, xs[3], ys[r]), X_MINUS + r, x_to[1]).wait_recv()
        if r in (0, 1):
            g_copy(p, block(p, xs[3], ys[r]), X_FAR + r, x_to[1]).start()
        g_copy(p, block(p, xs[1], ys[r]), X_PLUS + r, x_to[-1]).wait_recv()
        if r in (2, 3):
            g_copy(p, block(p, xs[1], ys[r]), X_FAR + r, x_to[-1]).start()

    def own_out(p):
        g_copy(p, block(p, x, y), Y_MINUS, y_to[1]).start()
        g_copy(p, block(p, x, y), Y_PLUS, y_to[-1]).start()
        send_x(p, 0)

    def y_pass(p):
        g_copy(p, block(p, x, ys[3]), Y_MINUS, y_to[1]).wait_recv()
        g_copy(p, y_half(p, ys[3], 0), Y_FAR_A, y_to[1]).start()
        send_x(p, 3)
        g_copy(p, block(p, x, ys[1]), Y_PLUS, y_to[-1]).wait_recv()
        g_copy(p, y_half(p, ys[1], 1), Y_FAR_B, y_to[-1]).start()
        send_x(p, 1)
        g_copy(p, y_half(p, ys[2], 0), Y_FAR_A, y_to[1]).wait_recv()
        g_copy(p, y_half(p, ys[2], 1), Y_FAR_B, y_to[-1]).wait_recv()
        send_x(p, 2)
        sib_line(p, 0).start()

    def x_pass(p):
        for r in (3, 1, 2):
            x_in(p, r)
        sib_line(p, 3).start()
        sib_line(p, 1).start()

    def x_far(p):
        for r in range(4):
            g_copy(p, block(p, xs[2], ys[r]), X_FAR + r, x_to[1]).wait_recv()
        sib_line(p, 2).start()

    def sib_in(p):
        for i in range(4):
            g_copy(p, gathered[p].at[xs[i], :, oc], SIB + i, sib).wait_recv()

    def gather_sent(p):
        g_copy(p, block(p, x, y), Y_MINUS, y_to[1]).wait_send()
        g_copy(p, block(p, x, y), Y_PLUS, y_to[-1]).wait_send()
        g_copy(p, y_half(p, ys[3], 0), Y_FAR_A, y_to[1]).wait_send()
        g_copy(p, y_half(p, ys[1], 1), Y_FAR_B, y_to[-1]).wait_send()
        for r in range(4):
            g_copy(p, block(p, x, ys[r]), X_MINUS + r, x_to[1]).wait_send()
            g_copy(p, block(p, x, ys[r]), X_PLUS + r, x_to[-1]).wait_send()
            g_copy(p, block(p, xs[3], ys[r]), X_FAR + r, x_to[1]).wait_send()
            sib_line(p, r).wait_send()

    def base_copy(p):
        src = gathered[p].at[x, y, c, :, pl.ds(0, D)]
        return copy(src, base_r.at[p], bs.at[p], br.at[p], dev(x, y, c, to[p]))

    def weights_of(p):
        meta = xf[:, :, :, :, pl.ds(D, META)].reshape(NX * NY * 2 * ROWS, META).astype(F32)
        lane = lax.broadcasted_iota(jnp.int32, meta.shape, 1) - (16 * p + x)
        picked = (lane == 0) | (lane == 4) | (lane == 8)
        weight = jnp.sum(jnp.where(picked, meta, 0.0), axis=1, keepdims=True)
        place = jnp.sum(jnp.where(lane == 12, meta, 0.0), axis=1, keepdims=True)
        return weight, place

    def rows_of(ref, k):
        return ref[:, :, :, :, pl.ds(k, KSTEP)].reshape(NX * NY * 2 * ROWS, KSTEP)

    def put(p, lo, value, weight):
        k, off = lo // C, lo % C
        value = (value * weight).reshape(NX, NY, 2, ROWS, SUB)
        parts[p][k, :, :, :, :, pl.ds(off, SUB)] = value
        sib_s[p, k, :, :, :, :, pl.ds(off, SUB)] = value.astype(BF)

    def c_copy(p, k, src, dst, sem, device):
        return copy(src, dst, cs.at[p, k, sem], cr.at[p, k, sem], device)

    def sib_out(p, k):
        return c_copy(p, k, sib_s.at[p, k, :, :, oc], sib_r.at[p, k], C_SIB, sib)

    def forward():
        acc = jnp.zeros((256, 2 * HID), F32)
        for k in range(0, D, KSTEP):
            acc = acc + dot(rows_of(xf, k), wcat[pl.ds(k, KSTEP), :])
        g, u = acc[:, :HID], acc[:, HID:]
        h = (g / (1.0 + jnp.exp(-g)) * u).astype(BF)
        weight, _ = weights_of(0)
        for k in range(NC):
            for lo in range(k * C, (k + 1) * C, SUB):
                put(0, lo, dot(h, wd[:, pl.ds(lo, SUB)]), weight)
            sib_out(0, k).start()

    def backward():
        dh = jnp.zeros((256, HID), F32)
        for k in range(0, D, KSTEP):
            dh = dh + dot_t(rows_of(xb, k), wd[:, pl.ds(k, KSTEP)])
        weight, place = weights_of(1)
        row = lax.broadcasted_iota(jnp.int32, (256, 1), 0)
        target = (row - row % 8).astype(F32) + place - 1.0
        target = jnp.where(place > 0.5, target, -1.0)
        col = lax.broadcasted_iota(jnp.int32, (256, 256), 1).astype(F32)
        pick = jnp.where(col == target, 1.0, 0.0).astype(BF)
        kept = dot(pick, saved[...].reshape(256, 2 * HID))
        a, b = kept[:, :HID], kept[:, HID:]
        sigma = 1.0 / (1.0 + jnp.exp(-a))
        dg = dh * b * (sigma * (1.0 + a * (1.0 - sigma)))
        du = dh * a * sigma
        dgu = jnp.concatenate([dg.astype(BF), du.astype(BF)], axis=1)
        for k in range(NC):
            for lo in range(k * C, (k + 1) * C, SUB):
                put(1, lo, dot_t(dgu, wcat[pl.ds(lo, SUB), :]), weight)
            sib_out(1, k).start()

    lower, upper = pl.ds(0, 2), pl.ds(2, 2)

    def both(p, k, xi, rows):
        return parts[p][k, xi, rows, c] + sib_r[p, k, xi, rows].astype(F32)

    def far(p, k, d):
        i = 0 if d > 0 else 1
        return c_copy(p, k, far_s.at[p, k, i], far_r.at[p, k, i], C_FAR_P + i, x_to[d])

    def near(p, k, d, rows, sem):
        i = 0 if d > 0 else 1
        return c_copy(p, k, near_s.at[p, k, i, rows], near_r.at[p, k, i, rows], sem + i, x_to[d])

    def x_one(p, k):
        sib_out(p, k).wait_recv()
        far_s[p, k, 0] = both(p, k, xs[2], lower).astype(BF)
        far(p, k, 1).start()
        far_s[p, k, 1] = both(p, k, xs[2], upper).astype(BF)
        far(p, k, -1).start()
        near_s[p, k, 0, upper] = both(p, k, xs[1], upper).astype(BF)
        near(p, k, 1, upper, C_ONE_P).start()
        near_s[p, k, 1, lower] = both(p, k, xs[3], lower).astype(BF)
        near(p, k, -1, lower, C_ONE_P).start()

    def x_two(p, k):
        far(p, k, 1).wait_recv()
        near_s[p, k, 0, lower] = (both(p, k, xs[1], lower) + far_r[p, k, 0].astype(F32)).astype(BF)
        near(p, k, 1, lower, C_TWO_P).start()
        far(p, k, -1).wait_recv()
        near_s[p, k, 1, upper] = (both(p, k, xs[3], upper) + far_r[p, k, 1].astype(F32)).astype(BF)
        near(p, k, -1, upper, C_TWO_P).start()

    def line(p, k, yi):
        mine = parts[p][k, x, yi, c] + sib_r[p, k, x, yi].astype(F32)
        return mine + near_r[p, k, 0, yi].astype(F32) + near_r[p, k, 1, yi].astype(F32)

    def y_far(p, k):
        return c_copy(p, k, yfar_s.at[p, k], yfar_r.at[p, k], C_YFAR, y_to[1 if k % 2 == 0 else -1])

    def y_near(p, k, d):
        i = 0 if d > 0 else 1
        device = dev(x, ys[1] if d > 0 else ys[3], c, to[p])
        return c_copy(p, k, ynear_s.at[p, k, i], ynear_r.at[p, k, i], C_Y_P + i, device)

    def y_own(p, k):
        return c_copy(p, k, own_s.at[p, k], own_r.at[p, k], C_OWN, dev(x, y, c, to[p]))

    def y_one(p, k):
        near(p, k, 1, upper, C_ONE_P).wait_recv()
        near(p, k, -1, lower, C_ONE_P).wait_recv()
        near(p, k, 1, lower, C_TWO_P).wait_recv()
        near(p, k, -1, upper, C_TWO_P).wait_recv()
        d = 1 if k % 2 == 0 else -1
        yfar_s[p, k] = line(p, k, ys[2]).astype(BF)
        y_far(p, k).start()
        ynear_s[p, k, 1 if d > 0 else 0] = line(p, k, ys[3] if d > 0 else ys[1]).astype(BF)
        y_near(p, k, -d).start()
        own_s[p, k] = line(p, k, y).astype(BF)
        y_own(p, k).start()

    def y_two(p, k):
        d = 1 if k % 2 == 0 else -1
        y_far(p, k).wait_recv()
        merged = line(p, k, ys[1] if d > 0 else ys[3]) + yfar_r[p, k].astype(F32)
        ynear_s[p, k, 0 if d > 0 else 1] = merged.astype(BF)
        y_near(p, k, d).start()

    def finish(p, k):
        y_own(p, k).wait_recv()
        y_near(p, k, 1).wait_recv()
        y_near(p, k, -1).wait_recv()
        cols = pl.ds(k * C, C)
        total = base_r[p, :, cols].astype(F32) + own_r[p, k].astype(F32)
        total = total + ynear_r[p, k, 0].astype(F32) + ynear_r[p, k, 1].astype(F32)
        outs[p][0, :, cols] = total.astype(BF)

    def combine_sent(p, k):
        sib_out(p, k).wait_send()
        for d in (1, -1):
            far(p, k, d).wait_send()
            near(p, k, d, lower, C_ONE_P if d < 0 else C_TWO_P).wait_send()
            near(p, k, d, upper, C_ONE_P if d > 0 else C_TWO_P).wait_send()
            y_near(p, k, d).wait_send()
        y_far(p, k).wait_send()
        y_own(p, k).wait_send()

    own_out(0)
    own_out(1)
    x_in(0, 0)
    y_pass(0)
    base_copy(0).start()
    base_copy(1).start()
    x_in(1, 0)
    y_pass(1)
    x_pass(0)
    x_far(0)
    x_pass(1)
    for load in loads[8:11]:
        load.wait()
    sib_in(0)
    forward()
    x_far(1)
    for k in range(NC):
        x_one(0, k)
    for k in range(NC):
        x_two(0, k)
    for load in loads[11:13]:
        load.wait()
    sib_in(1)
    backward()
    for k in range(NC):
        y_one(0, k)
    for k in range(NC):
        x_one(1, k)
    for k in range(NC):
        y_two(0, k)
    for k in range(NC):
        x_two(1, k)
    base_copy(0).wait_recv()
    for k in range(NC):
        finish(0, k)
    for k in range(NC):
        y_one(1, k)
    for k in range(NC):
        y_two(1, k)
    base_copy(1).wait_recv()
    for k in range(NC):
        finish(1, k)
    for p in range(2):
        gather_sent(p)
        base_copy(p).wait_send()
        for k in range(NC):
            combine_sent(p, k)


def local(*args):
    args = [a.transpose(0, 2, 1) if a.shape[-1] == 2 else a for a in args]
    out = jax.ShapeDtypeStruct((1, ROWS, D), BF)
    vm = pltpu.VMEM
    return pl.pallas_call(
        kernel,
        out_shape=(out, out),
        in_specs=[pl.BlockSpec(memory_space=pltpu.HBM)] * 13,
        out_specs=[pl.BlockSpec(memory_space=pltpu.VMEM)] * 2,
        scratch_shapes=[
            vm((NX, NY, 2, ROWS, D + META), BF),
            vm((NX, NY, 2, ROWS, D), BF),
            vm((D, 2 * HID), BF),
            vm((HID, D), BF),
            vm((32, 8, 2 * HID), BF),
            vm((4, 2, ROWS), jnp.int32),
            vm((2, 2, ROWS), F32),
            vm((NC, NX, NY, 2, ROWS, C), F32),
            vm((NC, NX, NY, 2, ROWS, C), F32),
            vm((2, NC, NX, NY, 2, ROWS, C), BF),
            vm((2, NC, NX, NY, ROWS, C), BF),
            vm((2, NC, 2, 2, ROWS, C), BF),
            vm((2, NC, 2, 2, ROWS, C), BF),
            vm((2, NC, 2, 4, ROWS, C), BF),
            vm((2, NC, 2, 4, ROWS, C), BF),
            vm((2, NC, ROWS, C), BF),
            vm((2, NC, ROWS, C), BF),
            vm((2, NC, 2, ROWS, C), BF),
            vm((2, NC, 2, ROWS, C), BF),
            vm((2, NC, ROWS, C), BF),
            vm((2, NC, ROWS, C), BF),
            vm((2, ROWS, D), BF),
            pltpu.SemaphoreType.DMA((2, N_GATHER)),
            pltpu.SemaphoreType.DMA((2, N_GATHER)),
            pltpu.SemaphoreType.DMA((2, NC, N_COMBINE)),
            pltpu.SemaphoreType.DMA((2, NC, N_COMBINE)),
            pltpu.SemaphoreType.DMA((2,)),
            pltpu.SemaphoreType.DMA((2,)),
            pltpu.SemaphoreType.DMA((13,)),
        ],
        compiler_params=pltpu.CompilerParams(
            collective_id=0, has_side_effects=True, vmem_limit_bytes=48 * 1024 * 1024
        ),
        cost_estimate=pl.CostEstimate(flops=1_500_000_000, bytes_accessed=4_000_000, transcendentals=70_000),
    )(*args)


def solution(mesh):
    tokens = P("section", "expert", None)
    saved = P("section", None, None, "expert")
    cols = P("section", None, "expert")
    in_specs = (tokens,) * 8 + (saved, saved, cols, cols, tokens)
    return jax.shard_map(local, mesh=mesh, in_specs=in_specs, out_specs=(tokens, tokens), check_vma=False)
```

```python
import jax
import jax.numpy as jnp
from jax import lax
from jax.experimental import pallas as pl
from jax.experimental.pallas import tpu as pltpu
from jax.sharding import PartitionSpec as P

NX, NY, NZ, ROWS, D, HID = 4, 4, 8, 8, 3584, 128
META = 128
HALF = D // 2
NC = 4
C = D // NC
KSTEP = 512
SUB = 896
BF, F32 = jnp.bfloat16, jnp.float32
X_DIRECT, Y_DIRECT = (2,), False
BASE_AT = (0, 0)
FAR_DIRECT, YFAR_DIRECT = False, True

Y_MINUS, Y_PLUS, Y_FAR_A, Y_FAR_B, X_MINUS, X_PLUS, X_FAR, SIB = 0, 1, 2, 3, 4, 8, 12, 16
N_GATHER = 20
C_SIB, C_FAR_P, C_FAR_M, C_ONE_P, C_ONE_M, C_TWO_P, C_TWO_M, C_YFAR, C_Y_P, C_Y_M, C_OWN = range(11)
N_COMBINE = 11


def dot(a, b):
    return lax.dot_general(a, b, (((1,), (0,)), ((), ())), preferred_element_type=F32)


def dot_t(a, b):
    return lax.dot_general(a, b, (((1,), (1,)), ((), ())), preferred_element_type=F32)


def routing_lanes(route, slot, weight, first):
    lane = lax.broadcasted_iota(jnp.int32, (ROWS, META), 1) - first
    square = (ROWS, ROWS)
    same = lax.broadcasted_iota(jnp.int32, square, 0) == lax.broadcasted_iota(jnp.int32, square, 1)

    def column(values, k):
        return jnp.sum(jnp.where(same, values[k : k + 1, :].astype(F32), 0.0), axis=1, keepdims=True)

    total = jnp.zeros((ROWS, META), F32)
    for k in range(2):
        expert = column(route, k).astype(jnp.int32)
        w = column(weight, k)
        hi = w.astype(BF).astype(F32)
        mid = (w - hi).astype(BF).astype(F32)
        low = w - hi - mid
        place = column(slot, k) + 1.0
        for i, part in enumerate((hi, mid, low, place)):
            total = total + jnp.where(lane == expert + 4 * i, part, 0.0)
    return total


def kernel(
    act, route_f, slot_f, weight_f, grad, route_b, slot_b, weight_b, saved_gate, saved_up, w_gate, w_up, w_down,
    out_f, out_b,
    xf, xb, wcat, wd, saved, ri, wi,
    part_f, part_b, sib_s, sib_r, far_s, far_r, near_s, near_r, yfar_s, yfar_r, ynear_s, ynear_r, own_s, own_r, base_r,
    hid, scale, z_sem, gs, gr, cs, cr, bs, br, ls,
):
    sec = lax.axis_index("section")
    ex = lax.axis_index("expert")
    nsec = lax.axis_size("section")
    x, y, c = ex // (NY * 2), (ex // 2) % NY, ex % 2
    oc = 1 - c
    xs = [(x + i) % NX for i in range(NX)]
    ys = [(y + i) % NY for i in range(NY)]
    to = [(sec + 1) % nsec, (sec + nsec - 1) % nsec]

    def dev(xi, yi, ci, s=sec):
        return (s, xi * (NY * 2) + yi * 2 + ci)

    def copy(src, dst, send, recv, device):
        return pltpu.make_async_remote_copy(
            src_ref=src, dst_ref=dst, send_sem=send, recv_sem=recv, device_id=device,
            device_id_type=pl.DeviceIdType.MESH,
        )

    sib = dev(x, y, oc)
    x_to = {1: dev(xs[1], y, c), -1: dev(xs[3], y, c)}
    y_to = {1: dev(x, ys[1], c), -1: dev(x, ys[3], c)}
    gathered = (xf, xb)
    widths = (D + META, D)
    parts = (part_f, part_b)
    outs = (out_f, out_b)

    loads = [
        pltpu.make_async_copy(act.at[0], xf.at[x, y, c, :, pl.ds(0, D)], ls.at[0]),
        pltpu.make_async_copy(grad.at[0], xb.at[x, y, c], ls.at[1]),
        pltpu.make_async_copy(route_f.at[0], ri.at[0], ls.at[2]),
        pltpu.make_async_copy(slot_f.at[0], ri.at[1], ls.at[3]),
        pltpu.make_async_copy(route_b.at[0], ri.at[2], ls.at[4]),
        pltpu.make_async_copy(slot_b.at[0], ri.at[3], ls.at[5]),
        pltpu.make_async_copy(weight_f.at[0], wi.at[0], ls.at[6]),
        pltpu.make_async_copy(weight_b.at[0], wi.at[1], ls.at[7]),
        pltpu.make_async_copy(w_gate.at[0], wcat.at[:, pl.ds(0, HID)], ls.at[8]),
        pltpu.make_async_copy(w_up.at[0], wcat.at[:, pl.ds(HID, HID)], ls.at[9]),
        pltpu.make_async_copy(w_down.at[0], wd, ls.at[10]),
        pltpu.make_async_copy(saved_gate.at[0], saved.at[:, :, pl.ds(0, HID)], ls.at[11]),
        pltpu.make_async_copy(saved_up.at[0], saved.at[:, :, pl.ds(HID, HID)], ls.at[12]),
    ]
    for load in loads:
        load.start()

    barrier = pltpu.get_barrier_semaphore()
    zi = sec % NZ
    near_devices = [sib, x_to[1], x_to[-1], dev(xs[2], y, c), y_to[1], y_to[-1], dev(x, ys[2], c)]
    after = [dev(x, yi, c, to[0]) for yi in ys]
    before = [dev(x, yi, c, to[1]) for yi in ys]

    def tell(sem, devices):
        for device in devices:
            pl.semaphore_signal(sem, inc=1, device_id=device, device_id_type=pl.DeviceIdType.MESH)

    tell(barrier, near_devices)

    @pl.when(zi < NZ - 1)
    def _():
        tell(barrier, after)

    @pl.when(zi == 0)
    def _():
        tell(barrier, before)

    for load in loads[2:8]:
        load.wait()
    lanes = routing_lanes(ri[0], ri[1], wi[0], 0) + routing_lanes(ri[2], ri[3], wi[1], 16)
    for load in loads[0:2]:
        load.wait()
    xf[x, y, c, :, pl.ds(D, META)] = lanes.astype(BF)
    def await_by_z(sem, first, middle, last):
        for here, amount in ((zi == 0, first), ((zi > 0) & (zi < NZ - 1), middle), (zi == NZ - 1, last)):
            if amount:

                @pl.when(here)
                def _():
                    pl.semaphore_wait(sem, amount)

    near_count = len(near_devices)
    await_by_z(barrier, near_count, near_count + NY, near_count + 2 * NY)

    @pl.when(zi > 0)
    def _():
        tell(z_sem, before)

    @pl.when(zi == NZ - 1)
    def _():
        tell(z_sem, after)

    def g_copy(p, ref, sem, device):
        return copy(ref, ref, gs.at[p, sem], gr.at[p, sem], device)

    def block(p, xi, yi):
        return gathered[p].at[xi, yi, c]

    def y_half(p, yi, half):
        cols = pl.ds(0, HALF) if half == 0 else pl.ds(HALF, widths[p] - HALF)
        return gathered[p].at[x, yi, c, :, cols]

    def sib_line(p, i):
        return g_copy(p, gathered[p].at[xs[i], :, c], SIB + i, sib)

    def send_x(p, r):
        g_copy(p, block(p, x, ys[r]), X_MINUS + r, x_to[1]).start()
        g_copy(p, block(p, x, ys[r]), X_PLUS + r, x_to[-1]).start()
        if r in X_DIRECT:
            g_copy(p, block(p, x, ys[r]), X_FAR + r, dev(xs[2], y, c)).start()

    def x_in(p, r):
        g_copy(p, block(p, xs[3], ys[r]), X_MINUS + r, x_to[1]).wait_recv()
        if r in (0, 1) and r not in X_DIRECT:
            g_copy(p, block(p, xs[3], ys[r]), X_FAR + r, x_to[1]).start()
        g_copy(p, block(p, xs[1], ys[r]), X_PLUS + r, x_to[-1]).wait_recv()
        if r in (2, 3) and r not in X_DIRECT:
            g_copy(p, block(p, xs[1], ys[r]), X_FAR + r, x_to[-1]).start()

    def own_y(p):
        g_copy(p, block(p, x, y), Y_MINUS, y_to[1]).start()
        g_copy(p, block(p, x, y), Y_PLUS, y_to[-1]).start()

    def y_in(p, d):
        i, r, sem, far_sem = (0, 3, Y_MINUS, Y_FAR_A) if d > 0 else (1, 1, Y_PLUS, Y_FAR_B)
        g_copy(p, block(p, x, ys[r]), sem, y_to[d]).wait_recv()
        g_copy(p, y_half(p, ys[r], i), far_sem, y_to[d]).start()
        send_x(p, r)

    def y_last(p):
        g_copy(p, y_half(p, ys[2], 0), Y_FAR_A, y_to[1]).wait_recv()
        g_copy(p, y_half(p, ys[2], 1), Y_FAR_B, y_to[-1]).wait_recv()
        send_x(p, 2)
        sib_line(p, 0).start()

    def sib_near(p):
        sib_line(p, 3).start()
        sib_line(p, 1).start()

    def x_far(p):
        for r in range(4):
            g_copy(p, block(p, xs[2], ys[r]), X_FAR + r, x_to[1]).wait_recv()
        sib_line(p, 2).start()

    def sib_in(p):
        for i in range(4):
            g_copy(p, gathered[p].at[xs[i], :, oc], SIB + i, sib).wait_recv()

    def gather_sent(p):
        g_copy(p, block(p, x, y), Y_MINUS, y_to[1]).wait_send()
        g_copy(p, block(p, x, y), Y_PLUS, y_to[-1]).wait_send()
        g_copy(p, y_half(p, ys[3], 0), Y_FAR_A, y_to[1]).wait_send()
        g_copy(p, y_half(p, ys[1], 1), Y_FAR_B, y_to[-1]).wait_send()
        for r in range(4):
            g_copy(p, block(p, x, ys[r]), X_MINUS + r, x_to[1]).wait_send()
            g_copy(p, block(p, x, ys[r]), X_PLUS + r, x_to[-1]).wait_send()
            g_copy(p, block(p, xs[3], ys[r]), X_FAR + r, x_to[1]).wait_send()
            sib_line(p, r).wait_send()

    def z_ready():
        await_by_z(z_sem, 2 * NY, NY, 0)

    def base_copy(p):
        src = gathered[p].at[x, y, c, :, pl.ds(0, D)]
        return copy(src, base_r.at[p], bs.at[p], br.at[p], dev(x, y, c, to[p]))

    def weights_of(p):
        meta = xf[:, :, :, :, pl.ds(D, META)].reshape(NX * NY * 2 * ROWS, META).astype(F32)
        lane = lax.broadcasted_iota(jnp.int32, meta.shape, 1) - (16 * p + x)
        picked = (lane == 0) | (lane == 4) | (lane == 8)
        weight = jnp.sum(jnp.where(picked, meta, 0.0), axis=1, keepdims=True)
        place = jnp.sum(jnp.where(lane == 12, meta, 0.0), axis=1, keepdims=True)
        return weight, place

    def rows_of(ref, k):
        return ref[:, :, :, :, pl.ds(k, KSTEP)].reshape(NX * NY * 2 * ROWS, KSTEP)

    def put(p, lo, value, weight):
        k, off = lo // C, lo % C
        value = (value * weight).reshape(NX, NY, 2, ROWS, SUB)
        parts[p][k, :, :, :, :, pl.ds(off, SUB)] = value
        sib_s[p, k, :, :, :, :, pl.ds(off, SUB)] = value.astype(BF)

    def c_copy(p, k, src, dst, sem, device):
        return copy(src, dst, cs.at[p, k, sem], cr.at[p, k, sem], device)

    def sib_out(p, k):
        return c_copy(p, k, sib_s.at[p, k, :, :, oc], sib_r.at[p, k], C_SIB, sib)

    def hidden_f():
        acc = jnp.zeros((256, 2 * HID), F32)
        for k in range(0, D, KSTEP):
            acc = acc + dot(rows_of(xf, k), wcat[pl.ds(k, KSTEP), :])
        g, u = acc[:, :HID], acc[:, HID:]
        hid[0, :, pl.ds(0, HID)] = (g / (1.0 + jnp.exp(-g)) * u).astype(BF)
        scale[0] = jnp.broadcast_to(weights_of(0)[0], (256, HID))

    def hidden_b():
        dh = jnp.zeros((256, HID), F32)
        for k in range(0, D, KSTEP):
            dh = dh + dot_t(rows_of(xb, k), wd[:, pl.ds(k, KSTEP)])
        weight, place = weights_of(1)
        row = lax.broadcasted_iota(jnp.int32, (256, 1), 0)
        target = (row - row % 8).astype(F32) + place - 1.0
        target = jnp.where(place > 0.5, target, -1.0)
        col = lax.broadcasted_iota(jnp.int32, (256, 256), 1).astype(F32)
        pick = jnp.where(col == target, 1.0, 0.0).astype(BF)
        kept = dot(pick, saved[...].reshape(256, 2 * HID))
        a, b = kept[:, :HID], kept[:, HID:]
        sigma = 1.0 / (1.0 + jnp.exp(-a))
        hid[1, :, pl.ds(0, HID)] = (dh * b * (sigma * (1.0 + a * (1.0 - sigma)))).astype(BF)
        hid[1, :, pl.ds(HID, HID)] = (dh * a * sigma).astype(BF)
        scale[1] = jnp.broadcast_to(weight, (256, HID))

    def hidden(p):
        for load in loads[8:11] if p == 0 else loads[11:13]:
            load.wait()
        sib_in(p)
        if p == 0:
            hidden_f()
        else:
            hidden_b()

    def outward(p, k):
        for lo in range(k * C, (k + 1) * C, SUB):
            if p == 0:
                value = dot(hid[0, :, pl.ds(0, HID)], wd[:, pl.ds(lo, SUB)])
            else:
                value = dot_t(hid[1], wcat[pl.ds(lo, SUB), :])
            put(p, lo, value, scale[p][:, :1])
        sib_out(p, k).start()

    lower, upper = pl.ds(0, 2), pl.ds(2, 2)

    def both(p, k, xi, rows):
        return parts[p][k, xi, rows, c] + sib_r[p, k, xi, rows].astype(F32)

    def far(p, k, d):
        i = 0 if d > 0 else 1
        return c_copy(p, k, far_s.at[p, k, i], far_r.at[p, k, i], C_FAR_P + i, dev(xs[2], y, c) if FAR_DIRECT else x_to[d])

    def near(p, k, d, rows, sem):
        i = 0 if d > 0 else 1
        return c_copy(p, k, near_s.at[p, k, i, rows], near_r.at[p, k, i, rows], sem + i, x_to[d])

    def x_one(p, k):
        sib_out(p, k).wait_recv()
        if FAR_DIRECT:
            for i, d in enumerate((1, -1)):
                near_s[p, k, i] = both(p, k, xs[d], slice(None)).astype(BF)
                near(p, k, d, lower, C_TWO_P).start()
                near(p, k, d, upper, C_ONE_P).start()
            far_s[p, k, 0] = both(p, k, xs[2], lower).astype(BF)
            far(p, k, 1).start()
            far_s[p, k, 1] = both(p, k, xs[2], upper).astype(BF)
            far(p, k, -1).start()
            return
        far_s[p, k, 0] = both(p, k, xs[2], lower).astype(BF)
        far(p, k, 1).start()
        far_s[p, k, 1] = both(p, k, xs[2], upper).astype(BF)
        far(p, k, -1).start()
        near_s[p, k, 0, upper] = both(p, k, xs[1], upper).astype(BF)
        near(p, k, 1, upper, C_ONE_P).start()
        near_s[p, k, 1, lower] = both(p, k, xs[3], lower).astype(BF)
        near(p, k, -1, lower, C_ONE_P).start()

    def x_two(p, k):
        if FAR_DIRECT:
            return
        far(p, k, 1).wait_recv()
        near_s[p, k, 0, lower] = (both(p, k, xs[1], lower) + far_r[p, k, 0].astype(F32)).astype(BF)
        near(p, k, 1, lower, C_TWO_P).start()
        far(p, k, -1).wait_recv()
        near_s[p, k, 1, upper] = (both(p, k, xs[3], upper) + far_r[p, k, 1].astype(F32)).astype(BF)
        near(p, k, -1, upper, C_TWO_P).start()

    def line(p, k, yi):
        mine = parts[p][k, x, yi, c] + sib_r[p, k, x, yi].astype(F32)
        if FAR_DIRECT:
            mine = mine + far_r[p, k, yi // 2, yi % 2].astype(F32)
        return mine + near_r[p, k, 0, yi].astype(F32) + near_r[p, k, 1, yi].astype(F32)

    def y_far(p, k):
        return c_copy(p, k, yfar_s.at[p, k], yfar_r.at[p, k], C_YFAR, dev(x, ys[2], c, to[p]) if YFAR_DIRECT else y_to[1 if k % 2 == 0 else -1])

    def y_near(p, k, d):
        i = 0 if d > 0 else 1
        device = dev(x, ys[1] if d > 0 else ys[3], c, to[p])
        return c_copy(p, k, ynear_s.at[p, k, i], ynear_r.at[p, k, i], C_Y_P + i, device)

    def y_own(p, k):
        return c_copy(p, k, own_s.at[p, k], own_r.at[p, k], C_OWN, dev(x, y, c, to[p]))

    def y_one(p, k):
        near(p, k, 1, upper, C_ONE_P).wait_recv()
        near(p, k, -1, lower, C_ONE_P).wait_recv()
        near(p, k, 1, lower, C_TWO_P).wait_recv()
        near(p, k, -1, upper, C_TWO_P).wait_recv()
        if FAR_DIRECT:
            far(p, k, 1).wait_recv()
            far(p, k, -1).wait_recv()
        if YFAR_DIRECT:
            for i, d in enumerate((1, -1)):
                ynear_s[p, k, i] = line(p, k, ys[d]).astype(BF)
                y_near(p, k, d).start()
            yfar_s[p, k] = line(p, k, ys[2]).astype(BF)
            y_far(p, k).start()
            own_s[p, k] = line(p, k, y).astype(BF)
            y_own(p, k).start()
            return
        d = 1 if k % 2 == 0 else -1
        yfar_s[p, k] = line(p, k, ys[2]).astype(BF)
        y_far(p, k).start()
        ynear_s[p, k, 1 if d > 0 else 0] = line(p, k, ys[3] if d > 0 else ys[1]).astype(BF)
        y_near(p, k, -d).start()
        own_s[p, k] = line(p, k, y).astype(BF)
        y_own(p, k).start()

    def y_two(p, k):
        if YFAR_DIRECT:
            return
        d = 1 if k % 2 == 0 else -1
        y_far(p, k).wait_recv()
        merged = line(p, k, ys[1] if d > 0 else ys[3]) + yfar_r[p, k].astype(F32)
        ynear_s[p, k, 0 if d > 0 else 1] = merged.astype(BF)
        y_near(p, k, d).start()

    def finish(p, k):
        if k == BASE_AT[p]:
            base_copy(p).wait_recv()
        y_own(p, k).wait_recv()
        y_near(p, k, 1).wait_recv()
        y_near(p, k, -1).wait_recv()
        if YFAR_DIRECT:
            y_far(p, k).wait_recv()
        cols = pl.ds(k * C, C)
        total = base_r[p, :, cols].astype(F32) + own_r[p, k].astype(F32)
        if YFAR_DIRECT:
            total = total + yfar_r[p, k].astype(F32)
        total = total + ynear_r[p, k, 0].astype(F32) + ynear_r[p, k, 1].astype(F32)
        outs[p][0, :, cols] = total.astype(BF)

    def combine_sent(p, k):
        sib_out(p, k).wait_send()
        for d in (1, -1):
            far(p, k, d).wait_send()
            near(p, k, d, lower, C_ONE_P if d < 0 else C_TWO_P).wait_send()
            near(p, k, d, upper, C_ONE_P if d > 0 else C_TWO_P).wait_send()
            y_near(p, k, d).wait_send()
        y_far(p, k).wait_send()
        y_own(p, k).wait_send()

    send_x(0, 0)
    own_y(0)
    x_in(0, 0)
    own_y(1)
    y_in(0, 1)
    send_x(1, 0)
    y_in(0, -1)
    y_in(1, -1)
    y_last(0)
    x_in(0, 1)
    x_in(0, 3)
    y_in(1, 1)
    y_last(1)
    x_in(0, 2)
    sib_near(0)
    x_far(0)
    x_in(1, 0)
    x_in(1, 3)
    x_in(1, 1)
    hidden(0)
    outward(0, 0)
    x_in(1, 2)
    outward(0, 1)
    outward(0, 2)
    x_one(0, 0)
    outward(0, 3)
    sib_near(1)
    x_one(0, 2)
    x_far(1)
    x_one(0, 1)
    x_one(0, 3)
    hidden(1)
    outward(1, 0)
    x_two(0, 0)
    x_two(0, 2)
    outward(1, 1)
    x_one(1, 0)
    outward(1, 2)
    outward(1, 3)
    x_two(0, 1)
    x_two(0, 3)
    x_one(1, 1)
    z_ready()
    base_copy(0).start()
    base_copy(1).start()
    y_one(0, 0)
    x_one(1, 3)
    y_one(0, 2)
    x_two(1, 0)
    y_one(0, 1)
    x_one(1, 2)
    y_one(0, 3)
    x_two(1, 1)
    x_two(1, 3)
    y_one(1, 0)
    x_two(1, 2)
    finish(0, 0)
    y_one(1, 1)
    finish(0, 1)
    finish(0, 2)
    y_one(1, 3)
    finish(0, 3)
    y_one(1, 2)
    finish(1, 0)
    finish(1, 3)
    finish(1, 1)
    finish(1, 2)
    for p in range(2):
        gather_sent(p)
        base_copy(p).wait_send()
        for k in range(NC):
            combine_sent(p, k)


def local(*args):
    args = [a.transpose(0, 2, 1) if a.shape[-1] == 2 else a for a in args]
    out = jax.ShapeDtypeStruct((1, ROWS, D), BF)
    vm = pltpu.VMEM
    return pl.pallas_call(
        kernel,
        out_shape=(out, out),
        in_specs=[pl.BlockSpec(memory_space=pltpu.HBM)] * 13,
        out_specs=[pl.BlockSpec(memory_space=pltpu.VMEM)] * 2,
        scratch_shapes=[
            vm((NX, NY, 2, ROWS, D + META), BF),
            vm((NX, NY, 2, ROWS, D), BF),
            vm((D, 2 * HID), BF),
            vm((HID, D), BF),
            vm((32, 8, 2 * HID), BF),
            vm((4, 2, ROWS), jnp.int32),
            vm((2, 2, ROWS), F32),
            vm((NC, NX, NY, 2, ROWS, C), F32),
            vm((NC, NX, NY, 2, ROWS, C), F32),
            vm((2, NC, NX, NY, 2, ROWS, C), BF),
            vm((2, NC, NX, NY, ROWS, C), BF),
            vm((2, NC, 2, 2, ROWS, C), BF),
            vm((2, NC, 2, 2, ROWS, C), BF),
            vm((2, NC, 2, 4, ROWS, C), BF),
            vm((2, NC, 2, 4, ROWS, C), BF),
            vm((2, NC, ROWS, C), BF),
            vm((2, NC, ROWS, C), BF),
            vm((2, NC, 2, ROWS, C), BF),
            vm((2, NC, 2, ROWS, C), BF),
            vm((2, NC, ROWS, C), BF),
            vm((2, NC, ROWS, C), BF),
            vm((2, ROWS, D), BF),
            vm((2, 256, 2 * HID), BF),
            vm((2, 256, HID), F32),
            pltpu.SemaphoreType.REGULAR,
            pltpu.SemaphoreType.DMA((2, N_GATHER)),
            pltpu.SemaphoreType.DMA((2, N_GATHER)),
            pltpu.SemaphoreType.DMA((2, NC, N_COMBINE)),
            pltpu.SemaphoreType.DMA((2, NC, N_COMBINE)),
            pltpu.SemaphoreType.DMA((2,)),
            pltpu.SemaphoreType.DMA((2,)),
            pltpu.SemaphoreType.DMA((13,)),
        ],
        compiler_params=pltpu.CompilerParams(
            collective_id=0, has_side_effects=True, vmem_limit_bytes=63 * 1024 * 1024
        ),
        cost_estimate=pl.CostEstimate(flops=1_500_000_000, bytes_accessed=4_000_000, transcendentals=70_000),
    )(*args)


def solution(mesh):
    tokens = P("section", "expert", None)
    saved = P("section", None, None, "expert")
    cols = P("section", None, "expert")
    in_specs = (tokens,) * 8 + (saved, saved, cols, cols, tokens)
    return jax.shard_map(local, mesh=mesh, in_specs=in_specs, out_specs=(tokens, tokens), check_vma=False)
```

```python
import jax
import jax.numpy as jnp
from jax import lax
from jax.experimental import pallas as pl
from jax.experimental.pallas import tpu as pltpu
from jax.sharding import PartitionSpec as P

NX, NY, NZ, ROWS, D, HID = 4, 4, 8, 8, 3584, 128
META = 128
HALF = D // 2
NC = 4
C = D // NC
KSTEP = 512
SUB = 896
BF, F32 = jnp.bfloat16, jnp.float32
X_DIRECT, Y_DIRECT = (2,), False
BASE_AT = (0, 0)
FAR_DIRECT, YFAR_DIRECT = False, True

Y_MINUS, Y_PLUS, Y_FAR_A, Y_FAR_B, X_MINUS, X_PLUS, X_FAR, SIB = 0, 1, 2, 3, 4, 8, 12, 16
N_GATHER = 20
C_SIB, C_FAR_P, C_FAR_M, C_ONE_P, C_ONE_M, C_TWO_P, C_TWO_M, C_YFAR, C_Y_P, C_Y_M, C_OWN = range(11)
N_COMBINE = 11


def dot(a, b):
    return lax.dot_general(a, b, (((1,), (0,)), ((), ())), preferred_element_type=F32)


def dot_t(a, b):
    return lax.dot_general(a, b, (((1,), (1,)), ((), ())), preferred_element_type=F32)


def routing_lanes(route, slot, weight, first):
    lane = lax.broadcasted_iota(jnp.int32, (ROWS, META), 1) - first
    square = (ROWS, ROWS)
    same = lax.broadcasted_iota(jnp.int32, square, 0) == lax.broadcasted_iota(jnp.int32, square, 1)

    def column(values, k):
        return jnp.sum(jnp.where(same, values[k : k + 1, :].astype(F32), 0.0), axis=1, keepdims=True)

    total = jnp.zeros((ROWS, META), F32)
    for k in range(2):
        expert = column(route, k).astype(jnp.int32)
        w = column(weight, k)
        hi = w.astype(BF).astype(F32)
        mid = (w - hi).astype(BF).astype(F32)
        low = w - hi - mid
        place = column(slot, k) + 1.0
        for i, part in enumerate((hi, mid, low, place)):
            total = total + jnp.where(lane == expert + 4 * i, part, 0.0)
    return total


def kernel(
    act, route_f, slot_f, weight_f, grad, route_b, slot_b, weight_b, saved_gate, saved_up, w_gate, w_up, w_down,
    out_f, out_b,
    xf, xb, wcat, wd, saved, ri, wi,
    part_f, part_b, sib_s, sib_r, far_s, far_r, near_s, near_r, yfar_s, yfar_r, ynear_s, ynear_r, own_s, own_r, base_r,
    hid, scale, z_sem, gs, gr, cs, cr, bs, br, ls,
):
    sec = lax.axis_index("section")
    ex = lax.axis_index("expert")
    nsec = lax.axis_size("section")
    x, y, c = ex // (NY * 2), (ex // 2) % NY, ex % 2
    oc = 1 - c
    xs = [(x + i) % NX for i in range(NX)]
    ys = [(y + i) % NY for i in range(NY)]
    to = [(sec + 1) % nsec, (sec + nsec - 1) % nsec]

    def dev(xi, yi, ci, s=sec):
        return (s, xi * (NY * 2) + yi * 2 + ci)

    def copy(src, dst, send, recv, device):
        return pltpu.make_async_remote_copy(
            src_ref=src, dst_ref=dst, send_sem=send, recv_sem=recv, device_id=device,
            device_id_type=pl.DeviceIdType.MESH,
        )

    sib = dev(x, y, oc)
    x_to = {1: dev(xs[1], y, c), -1: dev(xs[3], y, c)}
    y_to = {1: dev(x, ys[1], c), -1: dev(x, ys[3], c)}
    gathered = (xf, xb)
    widths = (D + META, D)
    parts = (part_f, part_b)
    outs = (out_f, out_b)

    loads = [
        pltpu.make_async_copy(act.at[0], xf.at[x, y, c, :, pl.ds(0, D)], ls.at[0]),
        pltpu.make_async_copy(grad.at[0], xb.at[x, y, c], ls.at[1]),
        pltpu.make_async_copy(route_f.at[0], ri.at[0], ls.at[2]),
        pltpu.make_async_copy(slot_f.at[0], ri.at[1], ls.at[3]),
        pltpu.make_async_copy(route_b.at[0], ri.at[2], ls.at[4]),
        pltpu.make_async_copy(slot_b.at[0], ri.at[3], ls.at[5]),
        pltpu.make_async_copy(weight_f.at[0], wi.at[0], ls.at[6]),
        pltpu.make_async_copy(weight_b.at[0], wi.at[1], ls.at[7]),
        pltpu.make_async_copy(w_gate.at[0], wcat.at[:, pl.ds(0, HID)], ls.at[8]),
        pltpu.make_async_copy(w_up.at[0], wcat.at[:, pl.ds(HID, HID)], ls.at[9]),
        pltpu.make_async_copy(w_down.at[0], wd, ls.at[10]),
        pltpu.make_async_copy(saved_gate.at[0], saved.at[:, :, pl.ds(0, HID)], ls.at[11]),
        pltpu.make_async_copy(saved_up.at[0], saved.at[:, :, pl.ds(HID, HID)], ls.at[12]),
    ]
    for load in loads:
        load.start()

    barrier = pltpu.get_barrier_semaphore()
    zi = sec % NZ
    near_devices = [sib, x_to[1], x_to[-1], dev(xs[2], y, c), y_to[1], y_to[-1], dev(x, ys[2], c)]
    after = [dev(x, yi, c, to[0]) for yi in ys]
    before = [dev(x, yi, c, to[1]) for yi in ys]

    def tell(sem, devices):
        for device in devices:
            pl.semaphore_signal(sem, inc=1, device_id=device, device_id_type=pl.DeviceIdType.MESH)

    tell(barrier, near_devices)

    @pl.when(zi < NZ - 1)
    def _():
        tell(barrier, after)

    @pl.when(zi == 0)
    def _():
        tell(barrier, before)

    for load in loads[2:8]:
        load.wait()
    lanes = routing_lanes(ri[0], ri[1], wi[0], 0) + routing_lanes(ri[2], ri[3], wi[1], 16)
    for load in loads[0:2]:
        load.wait()
    xf[x, y, c, :, pl.ds(D, META)] = lanes.astype(BF)
    def await_by_z(sem, first, middle, last):
        for here, amount in ((zi == 0, first), ((zi > 0) & (zi < NZ - 1), middle), (zi == NZ - 1, last)):
            if amount:

                @pl.when(here)
                def _():
                    pl.semaphore_wait(sem, amount)

    near_count = len(near_devices)
    await_by_z(barrier, near_count, near_count + NY, near_count + 2 * NY)

    @pl.when(zi > 0)
    def _():
        tell(z_sem, before)

    @pl.when(zi == NZ - 1)
    def _():
        tell(z_sem, after)

    def g_copy(p, ref, sem, device):
        return copy(ref, ref, gs.at[p, sem], gr.at[p, sem], device)

    def block(p, xi, yi):
        return gathered[p].at[xi, yi, c]

    def y_half(p, yi, half):
        cols = pl.ds(0, HALF) if half == 0 else pl.ds(HALF, widths[p] - HALF)
        return gathered[p].at[x, yi, c, :, cols]

    def sib_line(p, i):
        return g_copy(p, gathered[p].at[xs[i], :, c], SIB + i, sib)

    def send_x(p, r):
        g_copy(p, block(p, x, ys[r]), X_MINUS + r, x_to[1]).start()
        g_copy(p, block(p, x, ys[r]), X_PLUS + r, x_to[-1]).start()
        if r in X_DIRECT:
            g_copy(p, block(p, x, ys[r]), X_FAR + r, dev(xs[2], y, c)).start()

    def x_in(p, r):
        g_copy(p, block(p, xs[3], ys[r]), X_MINUS + r, x_to[1]).wait_recv()
        if r in (0, 1) and r not in X_DIRECT:
            g_copy(p, block(p, xs[3], ys[r]), X_FAR + r, x_to[1]).start()
        g_copy(p, block(p, xs[1], ys[r]), X_PLUS + r, x_to[-1]).wait_recv()
        if r in (2, 3) and r not in X_DIRECT:
            g_copy(p, block(p, xs[1], ys[r]), X_FAR + r, x_to[-1]).start()

    def own_y(p):
        g_copy(p, block(p, x, y), Y_MINUS, y_to[1]).start()
        g_copy(p, block(p, x, y), Y_PLUS, y_to[-1]).start()

    def y_in(p, d):
        i, r, sem, far_sem = (0, 3, Y_MINUS, Y_FAR_A) if d > 0 else (1, 1, Y_PLUS, Y_FAR_B)
        g_copy(p, block(p, x, ys[r]), sem, y_to[d]).wait_recv()
        g_copy(p, y_half(p, ys[r], i), far_sem, y_to[d]).start()
        send_x(p, r)

    def y_last(p):
        g_copy(p, y_half(p, ys[2], 0), Y_FAR_A, y_to[1]).wait_recv()
        g_copy(p, y_half(p, ys[2], 1), Y_FAR_B, y_to[-1]).wait_recv()
        send_x(p, 2)
        sib_line(p, 0).start()

    def sib_near(p):
        sib_line(p, 3).start()
        sib_line(p, 1).start()

    def x_far(p):
        for r in range(4):
            g_copy(p, block(p, xs[2], ys[r]), X_FAR + r, x_to[1]).wait_recv()
        sib_line(p, 2).start()

    def sib_in(p):
        for i in range(4):
            g_copy(p, gathered[p].at[xs[i], :, oc], SIB + i, sib).wait_recv()

    def gather_sent(p):
        g_copy(p, block(p, x, y), Y_MINUS, y_to[1]).wait_send()
        g_copy(p, block(p, x, y), Y_PLUS, y_to[-1]).wait_send()
        g_copy(p, y_half(p, ys[3], 0), Y_FAR_A, y_to[1]).wait_send()
        g_copy(p, y_half(p, ys[1], 1), Y_FAR_B, y_to[-1]).wait_send()
        for r in range(4):
            g_copy(p, block(p, x, ys[r]), X_MINUS + r, x_to[1]).wait_send()
            g_copy(p, block(p, x, ys[r]), X_PLUS + r, x_to[-1]).wait_send()
            g_copy(p, block(p, xs[3], ys[r]), X_FAR + r, x_to[1]).wait_send()
            sib_line(p, r).wait_send()

    def z_ready():
        await_by_z(z_sem, 2 * NY, NY, 0)

    def base_copy(p):
        src = gathered[p].at[x, y, c, :, pl.ds(0, D)]
        return copy(src, base_r.at[p], bs.at[p], br.at[p], dev(x, y, c, to[p]))

    def weights_of(p):
        meta = xf[:, :, :, :, pl.ds(D, META)].reshape(NX * NY * 2 * ROWS, META).astype(F32)
        lane = lax.broadcasted_iota(jnp.int32, meta.shape, 1) - (16 * p + x)
        picked = (lane == 0) | (lane == 4) | (lane == 8)
        weight = jnp.sum(jnp.where(picked, meta, 0.0), axis=1, keepdims=True)
        place = jnp.sum(jnp.where(lane == 12, meta, 0.0), axis=1, keepdims=True)
        return weight, place

    def rows_of(ref, k):
        return ref[:, :, :, :, pl.ds(k, KSTEP)].reshape(NX * NY * 2 * ROWS, KSTEP)

    def put(p, lo, value, weight):
        k, off = lo // C, lo % C
        value = (value * weight).reshape(NX, NY, 2, ROWS, SUB)
        parts[p][k, :, :, :, :, pl.ds(off, SUB)] = value
        sib_s[p, k, :, :, :, :, pl.ds(off, SUB)] = value.astype(BF)

    def c_copy(p, k, src, dst, sem, device):
        return copy(src, dst, cs.at[p, k, sem], cr.at[p, k, sem], device)

    def sib_out(p, k):
        return c_copy(p, k, sib_s.at[p, k, :, :, oc], sib_r.at[p, k], C_SIB, sib)

    def hidden_f():
        acc = jnp.zeros((256, 2 * HID), F32)
        for k in range(0, D, KSTEP):
            acc = acc + dot(rows_of(xf, k), wcat[pl.ds(k, KSTEP), :])
        g, u = acc[:, :HID], acc[:, HID:]
        hid[0, :, pl.ds(0, HID)] = (g / (1.0 + jnp.exp(-g)) * u).astype(BF)
        scale[0] = jnp.broadcast_to(weights_of(0)[0], (256, HID))

    def hidden_b():
        dh = jnp.zeros((256, HID), F32)
        for k in range(0, D, KSTEP):
            dh = dh + dot_t(rows_of(xb, k), wd[:, pl.ds(k, KSTEP)])
        weight, place = weights_of(1)
        row = lax.broadcasted_iota(jnp.int32, (256, 1), 0)
        target = (row - row % 8).astype(F32) + place - 1.0
        target = jnp.where(place > 0.5, target, -1.0)
        col = lax.broadcasted_iota(jnp.int32, (256, 256), 1).astype(F32)
        pick = jnp.where(col == target, 1.0, 0.0).astype(BF)
        kept = dot(pick, saved[...].reshape(256, 2 * HID))
        a, b = kept[:, :HID], kept[:, HID:]
        sigma = 1.0 / (1.0 + jnp.exp(-a))
        hid[1, :, pl.ds(0, HID)] = (dh * b * (sigma * (1.0 + a * (1.0 - sigma)))).astype(BF)
        hid[1, :, pl.ds(HID, HID)] = (dh * a * sigma).astype(BF)
        scale[1] = jnp.broadcast_to(weight, (256, HID))

    def hidden(p):
        for load in loads[8:11] if p == 0 else loads[11:13]:
            load.wait()
        sib_in(p)
        if p == 0:
            hidden_f()
        else:
            hidden_b()

    def outward(p, k):
        for lo in range(k * C, (k + 1) * C, SUB):
            if p == 0:
                value = dot(hid[0, :, pl.ds(0, HID)], wd[:, pl.ds(lo, SUB)])
            else:
                value = dot_t(hid[1], wcat[pl.ds(lo, SUB), :])
            put(p, lo, value, scale[p][:, :1])
        sib_out(p, k).start()

    lower, upper = pl.ds(0, 2), pl.ds(2, 2)

    def both(p, k, xi, rows):
        return parts[p][k, xi, rows, c] + sib_r[p, k, xi, rows].astype(F32)

    def far(p, k, d):
        i = 0 if d > 0 else 1
        return c_copy(p, k, far_s.at[p, k, i], far_r.at[p, k, i], C_FAR_P + i, dev(xs[2], y, c) if FAR_DIRECT else x_to[d])

    def near(p, k, d, rows, sem):
        i = 0 if d > 0 else 1
        return c_copy(p, k, near_s.at[p, k, i, rows], near_r.at[p, k, i, rows], sem + i, x_to[d])

    def x_one(p, k):
        sib_out(p, k).wait_recv()
        if FAR_DIRECT:
            for i, d in enumerate((1, -1)):
                near_s[p, k, i] = both(p, k, xs[d], slice(None)).astype(BF)
                near(p, k, d, lower, C_TWO_P).start()
                near(p, k, d, upper, C_ONE_P).start()
            far_s[p, k, 0] = both(p, k, xs[2], lower).astype(BF)
            far(p, k, 1).start()
            far_s[p, k, 1] = both(p, k, xs[2], upper).astype(BF)
            far(p, k, -1).start()
            return
        far_s[p, k, 0] = both(p, k, xs[2], lower).astype(BF)
        far(p, k, 1).start()
        far_s[p, k, 1] = both(p, k, xs[2], upper).astype(BF)
        far(p, k, -1).start()
        near_s[p, k, 0, upper] = both(p, k, xs[1], upper).astype(BF)
        near(p, k, 1, upper, C_ONE_P).start()
        near_s[p, k, 1, lower] = both(p, k, xs[3], lower).astype(BF)
        near(p, k, -1, lower, C_ONE_P).start()

    def x_two(p, k):
        if FAR_DIRECT:
            return
        far(p, k, 1).wait_recv()
        near_s[p, k, 0, lower] = (both(p, k, xs[1], lower) + far_r[p, k, 0].astype(F32)).astype(BF)
        near(p, k, 1, lower, C_TWO_P).start()
        far(p, k, -1).wait_recv()
        near_s[p, k, 1, upper] = (both(p, k, xs[3], upper) + far_r[p, k, 1].astype(F32)).astype(BF)
        near(p, k, -1, upper, C_TWO_P).start()

    def line(p, k, yi):
        mine = parts[p][k, x, yi, c] + sib_r[p, k, x, yi].astype(F32)
        if FAR_DIRECT:
            mine = mine + far_r[p, k, yi // 2, yi % 2].astype(F32)
        return mine + near_r[p, k, 0, yi].astype(F32) + near_r[p, k, 1, yi].astype(F32)

    def y_far(p, k):
        return c_copy(p, k, yfar_s.at[p, k], yfar_r.at[p, k], C_YFAR, dev(x, ys[2], c, to[p]) if YFAR_DIRECT else y_to[1 if k % 2 == 0 else -1])

    def y_near(p, k, d):
        i = 0 if d > 0 else 1
        device = dev(x, ys[1] if d > 0 else ys[3], c, to[p])
        return c_copy(p, k, ynear_s.at[p, k, i], ynear_r.at[p, k, i], C_Y_P + i, device)

    def y_own(p, k):
        return c_copy(p, k, own_s.at[p, k], own_r.at[p, k], C_OWN, dev(x, y, c, to[p]))

    def y_one(p, k):
        near(p, k, 1, upper, C_ONE_P).wait_recv()
        near(p, k, -1, lower, C_ONE_P).wait_recv()
        near(p, k, 1, lower, C_TWO_P).wait_recv()
        near(p, k, -1, upper, C_TWO_P).wait_recv()
        if FAR_DIRECT:
            far(p, k, 1).wait_recv()
            far(p, k, -1).wait_recv()
        if YFAR_DIRECT:
            for i, d in enumerate((1, -1)):
                ynear_s[p, k, i] = line(p, k, ys[d]).astype(BF)
                y_near(p, k, d).start()
            yfar_s[p, k] = line(p, k, ys[2]).astype(BF)
            y_far(p, k).start()
            own_s[p, k] = line(p, k, y).astype(BF)
            y_own(p, k).start()
            return
        d = 1 if k % 2 == 0 else -1
        yfar_s[p, k] = line(p, k, ys[2]).astype(BF)
        y_far(p, k).start()
        ynear_s[p, k, 1 if d > 0 else 0] = line(p, k, ys[3] if d > 0 else ys[1]).astype(BF)
        y_near(p, k, -d).start()
        own_s[p, k] = line(p, k, y).astype(BF)
        y_own(p, k).start()

    def y_two(p, k):
        if YFAR_DIRECT:
            return
        d = 1 if k % 2 == 0 else -1
        y_far(p, k).wait_recv()
        merged = line(p, k, ys[1] if d > 0 else ys[3]) + yfar_r[p, k].astype(F32)
        ynear_s[p, k, 0 if d > 0 else 1] = merged.astype(BF)
        y_near(p, k, d).start()

    def finish(p, k):
        if k == BASE_AT[p]:
            base_copy(p).wait_recv()
        y_own(p, k).wait_recv()
        y_near(p, k, 1).wait_recv()
        y_near(p, k, -1).wait_recv()
        if YFAR_DIRECT:
            y_far(p, k).wait_recv()
        cols = pl.ds(k * C, C)
        total = base_r[p, :, cols].astype(F32) + own_r[p, k].astype(F32)
        if YFAR_DIRECT:
            total = total + yfar_r[p, k].astype(F32)
        total = total + ynear_r[p, k, 0].astype(F32) + ynear_r[p, k, 1].astype(F32)
        outs[p][0, :, cols] = total.astype(BF)

    def combine_sent(p, k):
        sib_out(p, k).wait_send()
        for d in (1, -1):
            far(p, k, d).wait_send()
            near(p, k, d, lower, C_ONE_P if d < 0 else C_TWO_P).wait_send()
            near(p, k, d, upper, C_ONE_P if d > 0 else C_TWO_P).wait_send()
            y_near(p, k, d).wait_send()
        y_far(p, k).wait_send()
        y_own(p, k).wait_send()

    send_x(0, 0)
    own_y(0)
    x_in(0, 0)
    own_y(1)
    y_in(0, 1)
    send_x(1, 0)
    y_in(0, -1)
    y_in(1, -1)
    y_last(0)
    x_in(0, 1)
    x_in(0, 3)
    y_in(1, 1)
    y_last(1)
    x_in(0, 2)
    sib_near(0)
    x_far(0)
    x_in(1, 0)
    x_in(1, 3)
    x_in(1, 1)
    hidden(0)
    outward(0, 0)
    x_in(1, 2)
    outward(0, 1)
    outward(0, 2)
    x_one(0, 0)
    outward(0, 3)
    sib_near(1)
    x_one(0, 2)
    x_far(1)
    x_one(0, 1)
    x_one(0, 3)
    hidden(1)
    outward(1, 0)
    x_two(0, 0)
    x_two(0, 2)
    outward(1, 1)
    x_one(1, 0)
    outward(1, 2)
    outward(1, 3)
    x_two(0, 1)
    x_two(0, 3)
    x_one(1, 1)
    z_ready()
    base_copy(0).start()
    base_copy(1).start()
    y_one(0, 0)
    x_one(1, 3)
    y_one(0, 2)
    x_two(1, 0)
    y_one(0, 1)
    x_one(1, 2)
    y_one(0, 3)
    x_two(1, 1)
    x_two(1, 3)
    y_one(1, 0)
    x_two(1, 2)
    finish(0, 0)
    y_one(1, 1)
    finish(0, 1)
    finish(0, 2)
    y_one(1, 3)
    finish(0, 3)
    y_one(1, 2)
    finish(1, 0)
    finish(1, 3)
    finish(1, 1)
    finish(1, 2)
    for p in range(2):
        gather_sent(p)
        base_copy(p).wait_send()
        for k in range(NC):
            combine_sent(p, k)


def local(*args):
    args = [a.transpose(0, 2, 1) if a.shape[-1] == 2 else a for a in args]
    out = pltpu.VMEM((1, ROWS, D), BF)
    vm = pltpu.VMEM
    return pl.pallas_call(
        kernel,
        out_shape=(out, out),
        in_specs=[pl.BlockSpec(memory_space=pltpu.HBM)] * 13,
        out_specs=[pl.BlockSpec(memory_space=pltpu.VMEM)] * 2,
        scratch_shapes=[
            vm((NX, NY, 2, ROWS, D + META), BF),
            vm((NX, NY, 2, ROWS, D), BF),
            vm((D, 2 * HID), BF),
            vm((HID, D), BF),
            vm((32, 8, 2 * HID), BF),
            vm((4, 2, ROWS), jnp.int32),
            vm((2, 2, ROWS), F32),
            vm((NC, NX, NY, 2, ROWS, C), F32),
            vm((NC, NX, NY, 2, ROWS, C), F32),
            vm((2, NC, NX, NY, 2, ROWS, C), BF),
            vm((2, NC, NX, NY, ROWS, C), BF),
            vm((2, NC, 2, 2, ROWS, C), BF),
            vm((2, NC, 2, 2, ROWS, C), BF),
            vm((2, NC, 2, 4, ROWS, C), BF),
            vm((2, NC, 2, 4, ROWS, C), BF),
            vm((2, NC, ROWS, C), BF),
            vm((2, NC, ROWS, C), BF),
            vm((2, NC, 2, ROWS, C), BF),
            vm((2, NC, 2, ROWS, C), BF),
            vm((2, NC, ROWS, C), BF),
            vm((2, NC, ROWS, C), BF),
            vm((2, ROWS, D), BF),
            vm((2, 256, 2 * HID), BF),
            vm((2, 256, HID), F32),
            pltpu.SemaphoreType.REGULAR,
            pltpu.SemaphoreType.DMA((2, N_GATHER)),
            pltpu.SemaphoreType.DMA((2, N_GATHER)),
            pltpu.SemaphoreType.DMA((2, NC, N_COMBINE)),
            pltpu.SemaphoreType.DMA((2, NC, N_COMBINE)),
            pltpu.SemaphoreType.DMA((2,)),
            pltpu.SemaphoreType.DMA((2,)),
            pltpu.SemaphoreType.DMA((13,)),
        ],
        compiler_params=pltpu.CompilerParams(
            collective_id=0, has_side_effects=True, vmem_limit_bytes=63 * 1024 * 1024
        ),
        cost_estimate=pl.CostEstimate(flops=1_500_000_000, bytes_accessed=4_000_000, transcendentals=70_000),
    )(*args)


def solution(mesh):
    tokens = P("section", "expert", None)
    saved = P("section", None, None, "expert")
    cols = P("section", None, "expert")
    in_specs = (tokens,) * 8 + (saved, saved, cols, cols, tokens)
    return jax.shard_map(local, mesh=mesh, in_specs=in_specs, out_specs=(tokens, tokens), check_vma=False)
```

```python
import jax
import jax.numpy as jnp
from jax import lax
from jax.experimental import pallas as pl
from jax.experimental.pallas import tpu as pltpu
from jax.sharding import PartitionSpec as P

NX, NY, NZ, ROWS, D, HID = 4, 4, 8, 8, 3584, 128
META = 128
HALF = D // 2
NC = 4
C = D // NC
KSTEP = 512
SUB = 896
BF, F32 = jnp.bfloat16, jnp.float32
X_DIRECT, Y_DIRECT = (2,), False
BASE_AT = (0, 0)
FAR_DIRECT, YFAR_DIRECT = False, True

Y_MINUS, Y_PLUS, Y_FAR_A, Y_FAR_B, X_MINUS, X_PLUS, X_FAR, SIB = 0, 1, 2, 3, 4, 8, 12, 16
N_GATHER = 20
C_SIB, C_FAR_P, C_FAR_M, C_ONE_P, C_ONE_M, C_TWO_P, C_TWO_M, C_YFAR, C_Y_P, C_Y_M, C_OWN = range(11)
N_COMBINE = 11


def dot(a, b):
    return lax.dot_general(a, b, (((1,), (0,)), ((), ())), preferred_element_type=F32)


def dot_t(a, b):
    return lax.dot_general(a, b, (((1,), (1,)), ((), ())), preferred_element_type=F32)


def routing_lanes(route, slot, weight, first):
    lane = lax.broadcasted_iota(jnp.int32, (ROWS, META), 1) - first
    square = (ROWS, ROWS)
    same = lax.broadcasted_iota(jnp.int32, square, 0) == lax.broadcasted_iota(jnp.int32, square, 1)

    def column(values, k):
        return jnp.sum(jnp.where(same, values[k : k + 1, :].astype(F32), 0.0), axis=1, keepdims=True)

    total = jnp.zeros((ROWS, META), F32)
    for k in range(2):
        expert = column(route, k).astype(jnp.int32)
        w = column(weight, k)
        hi = w.astype(BF).astype(F32)
        mid = (w - hi).astype(BF).astype(F32)
        low = w - hi - mid
        place = column(slot, k) + 1.0
        for i, part in enumerate((hi, mid, low, place)):
            total = total + jnp.where(lane == expert + 4 * i, part, 0.0)
    return total


def kernel(
    act, route_f, slot_f, weight_f, grad, route_b, slot_b, weight_b, saved_gate, saved_up, w_gate, w_up, w_down,
    out_f, out_b,
    xf, xb, wcat, wd, saved, ri, wi,
    part_f, part_b, sib_s, sib_r, far_s, far_r, near_s, near_r, yfar_s, yfar_r, ynear_s, ynear_r, own_s, own_r, base_r,
    hid, scale, z_sem, gs, gr, cs, cr, bs, br, ls,
):
    sec = lax.axis_index("section")
    ex = lax.axis_index("expert")
    nsec = lax.axis_size("section")
    x, y, c = ex // (NY * 2), (ex // 2) % NY, ex % 2
    oc = 1 - c
    xs = [(x + i) % NX for i in range(NX)]
    ys = [(y + i) % NY for i in range(NY)]
    to = [(sec + 1) % nsec, (sec + nsec - 1) % nsec]

    def dev(xi, yi, ci, s=sec):
        return (s, xi * (NY * 2) + yi * 2 + ci)

    def copy(src, dst, send, recv, device):
        return pltpu.make_async_remote_copy(
            src_ref=src, dst_ref=dst, send_sem=send, recv_sem=recv, device_id=device,
            device_id_type=pl.DeviceIdType.MESH,
        )

    sib = dev(x, y, oc)
    x_to = {1: dev(xs[1], y, c), -1: dev(xs[3], y, c)}
    y_to = {1: dev(x, ys[1], c), -1: dev(x, ys[3], c)}
    gathered = (xf, xb)
    widths = (D + META, D)
    parts = (part_f, part_b)
    outs = (out_f, out_b)

    loads = [
        pltpu.make_async_copy(act.at[0], xf.at[x, y, c, :, pl.ds(0, D)], ls.at[0]),
        pltpu.make_async_copy(grad.at[0], xb.at[x, y, c], ls.at[1]),
        pltpu.make_async_copy(route_f.at[0], ri.at[0], ls.at[2]),
        pltpu.make_async_copy(slot_f.at[0], ri.at[1], ls.at[3]),
        pltpu.make_async_copy(route_b.at[0], ri.at[2], ls.at[4]),
        pltpu.make_async_copy(slot_b.at[0], ri.at[3], ls.at[5]),
        pltpu.make_async_copy(weight_f.at[0], wi.at[0], ls.at[6]),
        pltpu.make_async_copy(weight_b.at[0], wi.at[1], ls.at[7]),
        pltpu.make_async_copy(w_gate.at[0], wcat.at[:, pl.ds(0, HID)], ls.at[8]),
        pltpu.make_async_copy(w_up.at[0], wcat.at[:, pl.ds(HID, HID)], ls.at[9]),
        pltpu.make_async_copy(w_down.at[0], wd, ls.at[10]),
        pltpu.make_async_copy(saved_gate.at[0], saved.at[:, :, pl.ds(0, HID)], ls.at[11]),
        pltpu.make_async_copy(saved_up.at[0], saved.at[:, :, pl.ds(HID, HID)], ls.at[12]),
    ]
    for load in loads:
        load.start()

    barrier = pltpu.get_barrier_semaphore()
    zi = sec % NZ
    near_devices = [sib, x_to[1], x_to[-1], dev(xs[2], y, c), y_to[1], y_to[-1], dev(x, ys[2], c)]
    after = [dev(x, yi, c, to[0]) for yi in ys]
    before = [dev(x, yi, c, to[1]) for yi in ys]

    def tell(sem, devices):
        for device in devices:
            pl.semaphore_signal(sem, inc=1, device_id=device, device_id_type=pl.DeviceIdType.MESH)

    tell(barrier, near_devices)

    @pl.when(zi < NZ - 1)
    def _():
        tell(barrier, after)

    @pl.when(zi == 0)
    def _():
        tell(barrier, before)

    for load in loads[2:8]:
        load.wait()
    lanes = routing_lanes(ri[0], ri[1], wi[0], 0) + routing_lanes(ri[2], ri[3], wi[1], 16)
    for load in loads[0:2]:
        load.wait()
    xf[x, y, c, :, pl.ds(D, META)] = lanes.astype(BF)
    def await_by_z(sem, first, middle, last):
        for here, amount in ((zi == 0, first), ((zi > 0) & (zi < NZ - 1), middle), (zi == NZ - 1, last)):
            if amount:

                @pl.when(here)
                def _():
                    pl.semaphore_wait(sem, amount)

    near_count = len(near_devices)
    await_by_z(barrier, near_count, near_count + NY, near_count + 2 * NY)

    @pl.when(zi > 0)
    def _():
        tell(z_sem, before)

    @pl.when(zi == NZ - 1)
    def _():
        tell(z_sem, after)

    def g_copy(p, ref, sem, device):
        return copy(ref, ref, gs.at[p, sem], gr.at[p, sem], device)

    def block(p, xi, yi):
        return gathered[p].at[xi, yi, c]

    def y_half(p, yi, half):
        cols = pl.ds(0, HALF) if half == 0 else pl.ds(HALF, widths[p] - HALF)
        return gathered[p].at[x, yi, c, :, cols]

    def sib_line(p, i):
        return g_copy(p, gathered[p].at[xs[i], :, c], SIB + i, sib)

    def send_x(p, r):
        g_copy(p, block(p, x, ys[r]), X_MINUS + r, x_to[1]).start()
        g_copy(p, block(p, x, ys[r]), X_PLUS + r, x_to[-1]).start()
        if r in X_DIRECT:
            g_copy(p, block(p, x, ys[r]), X_FAR + r, dev(xs[2], y, c)).start()

    def x_in(p, r):
        g_copy(p, block(p, xs[3], ys[r]), X_MINUS + r, x_to[1]).wait_recv()
        if r in (0, 1) and r not in X_DIRECT:
            g_copy(p, block(p, xs[3], ys[r]), X_FAR + r, x_to[1]).start()
        g_copy(p, block(p, xs[1], ys[r]), X_PLUS + r, x_to[-1]).wait_recv()
        if r in (2, 3) and r not in X_DIRECT:
            g_copy(p, block(p, xs[1], ys[r]), X_FAR + r, x_to[-1]).start()

    def own_y(p):
        g_copy(p, block(p, x, y), Y_MINUS, y_to[1]).start()
        g_copy(p, block(p, x, y), Y_PLUS, y_to[-1]).start()

    def y_in(p, d):
        i, r, sem, far_sem = (0, 3, Y_MINUS, Y_FAR_A) if d > 0 else (1, 1, Y_PLUS, Y_FAR_B)
        g_copy(p, block(p, x, ys[r]), sem, y_to[d]).wait_recv()
        g_copy(p, y_half(p, ys[r], i), far_sem, y_to[d]).start()
        send_x(p, r)

    def y_last(p):
        g_copy(p, y_half(p, ys[2], 0), Y_FAR_A, y_to[1]).wait_recv()
        g_copy(p, y_half(p, ys[2], 1), Y_FAR_B, y_to[-1]).wait_recv()
        send_x(p, 2)
        sib_line(p, 0).start()

    def sib_near(p):
        sib_line(p, 3).start()
        sib_line(p, 1).start()

    def x_far(p):
        for r in range(4):
            g_copy(p, block(p, xs[2], ys[r]), X_FAR + r, x_to[1]).wait_recv()
        sib_line(p, 2).start()

    def sib_in(p):
        for i in range(4):
            g_copy(p, gathered[p].at[xs[i], :, oc], SIB + i, sib).wait_recv()

    def gather_sent(p):
        g_copy(p, block(p, x, y), Y_MINUS, y_to[1]).wait_send()
        g_copy(p, block(p, x, y), Y_PLUS, y_to[-1]).wait_send()
        g_copy(p, y_half(p, ys[3], 0), Y_FAR_A, y_to[1]).wait_send()
        g_copy(p, y_half(p, ys[1], 1), Y_FAR_B, y_to[-1]).wait_send()
        for r in range(4):
            g_copy(p, block(p, x, ys[r]), X_MINUS + r, x_to[1]).wait_send()
            g_copy(p, block(p, x, ys[r]), X_PLUS + r, x_to[-1]).wait_send()
            g_copy(p, block(p, xs[3], ys[r]), X_FAR + r, x_to[1]).wait_send()
            sib_line(p, r).wait_send()

    def z_ready():
        await_by_z(z_sem, 2 * NY, NY, 0)

    def base_copy(p):
        src = gathered[p].at[x, y, c, :, pl.ds(0, D)]
        return copy(src, base_r.at[p], bs.at[p], br.at[p], dev(x, y, c, to[p]))

    def weights_of(p):
        meta = xf[:, :, :, :, pl.ds(D, META)].reshape(NX * NY * 2 * ROWS, META).astype(F32)
        lane = lax.broadcasted_iota(jnp.int32, meta.shape, 1) - (16 * p + x)
        picked = (lane == 0) | (lane == 4) | (lane == 8)
        weight = jnp.sum(jnp.where(picked, meta, 0.0), axis=1, keepdims=True)
        place = jnp.sum(jnp.where(lane == 12, meta, 0.0), axis=1, keepdims=True)
        return weight, place

    def rows_of(ref, k):
        return ref[:, :, :, :, pl.ds(k, KSTEP)].reshape(NX * NY * 2 * ROWS, KSTEP)

    def put(p, lo, value, weight):
        k, off = lo // C, lo % C
        value = (value * weight).reshape(NX, NY, 2, ROWS, SUB)
        parts[p][k, :, :, :, :, pl.ds(off, SUB)] = value
        sib_s[p, k, :, :, :, :, pl.ds(off, SUB)] = value.astype(BF)

    def c_copy(p, k, src, dst, sem, device):
        return copy(src, dst, cs.at[p, k, sem], cr.at[p, k, sem], device)

    def sib_out(p, k):
        return c_copy(p, k, sib_s.at[p, k, :, :, oc], sib_r.at[p, k], C_SIB, sib)

    def hidden_f():
        acc = jnp.zeros((256, 2 * HID), F32)
        for k in range(0, D, KSTEP):
            acc = acc + dot(rows_of(xf, k), wcat[pl.ds(k, KSTEP), :])
        g, u = acc[:, :HID], acc[:, HID:]
        hid[0, :, pl.ds(0, HID)] = (g / (1.0 + jnp.exp(-g)) * u).astype(BF)
        scale[0] = jnp.broadcast_to(weights_of(0)[0], (256, HID))

    def hidden_b():
        dh = jnp.zeros((256, HID), F32)
        for k in range(0, D, KSTEP):
            dh = dh + dot_t(rows_of(xb, k), wd[:, pl.ds(k, KSTEP)])
        weight, place = weights_of(1)
        row = lax.broadcasted_iota(jnp.int32, (256, 1), 0)
        target = (row - row % 8).astype(F32) + place - 1.0
        target = jnp.where(place > 0.5, target, -1.0)
        col = lax.broadcasted_iota(jnp.int32, (256, 256), 1).astype(F32)
        pick = jnp.where(col == target, 1.0, 0.0).astype(BF)
        kept = dot(pick, saved[...].reshape(256, 2 * HID))
        a, b = kept[:, :HID], kept[:, HID:]
        sigma = 1.0 / (1.0 + jnp.exp(-a))
        hid[1, :, pl.ds(0, HID)] = (dh * b * (sigma * (1.0 + a * (1.0 - sigma)))).astype(BF)
        hid[1, :, pl.ds(HID, HID)] = (dh * a * sigma).astype(BF)
        scale[1] = jnp.broadcast_to(weight, (256, HID))

    def hidden(p):
        for load in loads[8:11] if p == 0 else loads[11:13]:
            load.wait()
        sib_in(p)
        if p == 0:
            hidden_f()
        else:
            hidden_b()

    def outward(p, k):
        for lo in range(k * C, (k + 1) * C, SUB):
            if p == 0:
                value = dot(hid[0, :, pl.ds(0, HID)], wd[:, pl.ds(lo, SUB)])
            else:
                value = dot_t(hid[1], wcat[pl.ds(lo, SUB), :])
            put(p, lo, value, scale[p][:, :1])
        sib_out(p, k).start()

    lower, upper = pl.ds(0, 2), pl.ds(2, 2)

    def both(p, k, xi, rows):
        return parts[p][k, xi, rows, c] + sib_r[p, k, xi, rows].astype(F32)

    def far(p, k, d):
        i = 0 if d > 0 else 1
        return c_copy(p, k, far_s.at[p, k, i], far_r.at[p, k, i], C_FAR_P + i, dev(xs[2], y, c) if FAR_DIRECT else x_to[d])

    def near(p, k, d, rows, sem):
        i = 0 if d > 0 else 1
        return c_copy(p, k, near_s.at[p, k, i, rows], near_r.at[p, k, i, rows], sem + i, x_to[d])

    def x_one(p, k):
        sib_out(p, k).wait_recv()
        if FAR_DIRECT:
            for i, d in enumerate((1, -1)):
                near_s[p, k, i] = both(p, k, xs[d], slice(None)).astype(BF)
                near(p, k, d, lower, C_TWO_P).start()
                near(p, k, d, upper, C_ONE_P).start()
            far_s[p, k, 0] = both(p, k, xs[2], lower).astype(BF)
            far(p, k, 1).start()
            far_s[p, k, 1] = both(p, k, xs[2], upper).astype(BF)
            far(p, k, -1).start()
            return
        far_s[p, k, 0] = both(p, k, xs[2], lower).astype(BF)
        far(p, k, 1).start()
        far_s[p, k, 1] = both(p, k, xs[2], upper).astype(BF)
        far(p, k, -1).start()
        near_s[p, k, 0, upper] = both(p, k, xs[1], upper).astype(BF)
        near(p, k, 1, upper, C_ONE_P).start()
        near_s[p, k, 1, lower] = both(p, k, xs[3], lower).astype(BF)
        near(p, k, -1, lower, C_ONE_P).start()

    def x_two(p, k):
        if FAR_DIRECT:
            return
        far(p, k, 1).wait_recv()
        near_s[p, k, 0, lower] = (both(p, k, xs[1], lower) + far_r[p, k, 0].astype(F32)).astype(BF)
        near(p, k, 1, lower, C_TWO_P).start()
        far(p, k, -1).wait_recv()
        near_s[p, k, 1, upper] = (both(p, k, xs[3], upper) + far_r[p, k, 1].astype(F32)).astype(BF)
        near(p, k, -1, upper, C_TWO_P).start()

    def line(p, k, yi):
        mine = parts[p][k, x, yi, c] + sib_r[p, k, x, yi].astype(F32)
        if FAR_DIRECT:
            mine = mine + far_r[p, k, yi // 2, yi % 2].astype(F32)
        return mine + near_r[p, k, 0, yi].astype(F32) + near_r[p, k, 1, yi].astype(F32)

    def y_far(p, k):
        return c_copy(p, k, yfar_s.at[p, k], yfar_r.at[p, k], C_YFAR, dev(x, ys[2], c, to[p]) if YFAR_DIRECT else y_to[1 if k % 2 == 0 else -1])

    def y_near(p, k, d):
        i = 0 if d > 0 else 1
        device = dev(x, ys[1] if d > 0 else ys[3], c, to[p])
        return c_copy(p, k, ynear_s.at[p, k, i], ynear_r.at[p, k, i], C_Y_P + i, device)

    def y_own(p, k):
        return c_copy(p, k, own_s.at[p, k], own_r.at[p, k], C_OWN, dev(x, y, c, to[p]))

    def y_one(p, k):
        near(p, k, 1, upper, C_ONE_P).wait_recv()
        near(p, k, -1, lower, C_ONE_P).wait_recv()
        near(p, k, 1, lower, C_TWO_P).wait_recv()
        near(p, k, -1, upper, C_TWO_P).wait_recv()
        if FAR_DIRECT:
            far(p, k, 1).wait_recv()
            far(p, k, -1).wait_recv()
        if YFAR_DIRECT:
            for i, d in enumerate((1, -1)):
                ynear_s[p, k, i] = line(p, k, ys[d]).astype(BF)
                y_near(p, k, d).start()
            yfar_s[p, k] = line(p, k, ys[2]).astype(BF)
            y_far(p, k).start()
            own_s[p, k] = line(p, k, y).astype(BF)
            y_own(p, k).start()
            return
        d = 1 if k % 2 == 0 else -1
        yfar_s[p, k] = line(p, k, ys[2]).astype(BF)
        y_far(p, k).start()
        ynear_s[p, k, 1 if d > 0 else 0] = line(p, k, ys[3] if d > 0 else ys[1]).astype(BF)
        y_near(p, k, -d).start()
        own_s[p, k] = line(p, k, y).astype(BF)
        y_own(p, k).start()

    def y_two(p, k):
        if YFAR_DIRECT:
            return
        d = 1 if k % 2 == 0 else -1
        y_far(p, k).wait_recv()
        merged = line(p, k, ys[1] if d > 0 else ys[3]) + yfar_r[p, k].astype(F32)
        ynear_s[p, k, 0 if d > 0 else 1] = merged.astype(BF)
        y_near(p, k, d).start()

    def finish(p, k):
        if k == BASE_AT[p]:
            base_copy(p).wait_recv()
        y_own(p, k).wait_recv()
        y_near(p, k, 1).wait_recv()
        y_near(p, k, -1).wait_recv()
        if YFAR_DIRECT:
            y_far(p, k).wait_recv()
        cols = pl.ds(k * C, C)
        total = base_r[p, :, cols].astype(F32) + own_r[p, k].astype(F32)
        if YFAR_DIRECT:
            total = total + yfar_r[p, k].astype(F32)
        total = total + ynear_r[p, k, 0].astype(F32) + ynear_r[p, k, 1].astype(F32)
        outs[p][0, :, cols] = total.astype(BF)

    def combine_sent(p, k):
        sib_out(p, k).wait_send()
        for d in (1, -1):
            far(p, k, d).wait_send()
            near(p, k, d, lower, C_ONE_P if d < 0 else C_TWO_P).wait_send()
            near(p, k, d, upper, C_ONE_P if d > 0 else C_TWO_P).wait_send()
            y_near(p, k, d).wait_send()
        y_far(p, k).wait_send()
        y_own(p, k).wait_send()

    send_x(0, 0)
    own_y(0)
    x_in(0, 0)
    own_y(1)
    y_in(0, 1)
    send_x(1, 0)
    y_in(0, -1)
    y_in(1, -1)
    y_last(0)
    x_in(0, 1)
    x_in(0, 3)
    y_in(1, 1)
    x_in(0, 2)
    sib_near(0)
    y_last(1)
    x_in(1, 0)
    x_far(0)
    x_in(1, 1)
    x_in(1, 3)
    hidden(0)
    outward(0, 0)
    outward(0, 1)
    x_in(1, 2)
    outward(0, 2)
    x_one(0, 0)
    outward(0, 3)
    sib_near(1)
    x_one(0, 1)
    x_far(1)
    x_one(0, 2)
    x_one(0, 3)
    hidden(1)
    outward(1, 0)
    x_two(0, 0)
    x_two(0, 1)
    outward(1, 1)
    x_one(1, 0)
    outward(1, 2)
    x_two(0, 2)
    x_two(0, 3)
    x_one(1, 1)
    outward(1, 3)
    z_ready()
    base_copy(0).start()
    base_copy(1).start()
    y_one(0, 0)
    x_one(1, 2)
    y_one(0, 1)
    x_two(1, 0)
    x_one(1, 3)
    y_one(0, 2)
    x_two(1, 1)
    y_one(0, 3)
    x_two(1, 2)
    y_one(1, 0)
    x_two(1, 3)
    y_one(1, 1)
    y_one(1, 2)
    y_one(1, 3)
    finish(0, 0)
    finish(0, 1)
    finish(0, 2)
    finish(0, 3)
    finish(1, 0)
    finish(1, 1)
    finish(1, 2)
    finish(1, 3)
    for p in range(2):
        gather_sent(p)
        base_copy(p).wait_send()
        for k in range(NC):
            combine_sent(p, k)


def local(*args):
    args = [a.transpose(0, 2, 1) if a.shape[-1] == 2 else a for a in args]
    out = pltpu.VMEM((1, ROWS, D), BF)
    vm = pltpu.VMEM
    return pl.pallas_call(
        kernel,
        out_shape=(out, out),
        in_specs=[pl.BlockSpec(memory_space=pltpu.HBM)] * 13,
        out_specs=[pl.BlockSpec(memory_space=pltpu.VMEM)] * 2,
        scratch_shapes=[
            vm((NX, NY, 2, ROWS, D + META), BF),
            vm((NX, NY, 2, ROWS, D), BF),
            vm((D, 2 * HID), BF),
            vm((HID, D), BF),
            vm((32, 8, 2 * HID), BF),
            vm((4, 2, ROWS), jnp.int32),
            vm((2, 2, ROWS), F32),
            vm((NC, NX, NY, 2, ROWS, C), F32),
            vm((NC, NX, NY, 2, ROWS, C), F32),
            vm((2, NC, NX, NY, 2, ROWS, C), BF),
            vm((2, NC, NX, NY, ROWS, C), BF),
            vm((2, NC, 2, 2, ROWS, C), BF),
            vm((2, NC, 2, 2, ROWS, C), BF),
            vm((2, NC, 2, 4, ROWS, C), BF),
            vm((2, NC, 2, 4, ROWS, C), BF),
            vm((2, NC, ROWS, C), BF),
            vm((2, NC, ROWS, C), BF),
            vm((2, NC, 2, ROWS, C), BF),
            vm((2, NC, 2, ROWS, C), BF),
            vm((2, NC, ROWS, C), BF),
            vm((2, NC, ROWS, C), BF),
            vm((2, ROWS, D), BF),
            vm((2, 256, 2 * HID), BF),
            vm((2, 256, HID), F32),
            pltpu.SemaphoreType.REGULAR,
            pltpu.SemaphoreType.DMA((2, N_GATHER)),
            pltpu.SemaphoreType.DMA((2, N_GATHER)),
            pltpu.SemaphoreType.DMA((2, NC, N_COMBINE)),
            pltpu.SemaphoreType.DMA((2, NC, N_COMBINE)),
            pltpu.SemaphoreType.DMA((2,)),
            pltpu.SemaphoreType.DMA((2,)),
            pltpu.SemaphoreType.DMA((13,)),
        ],
        compiler_params=pltpu.CompilerParams(
            collective_id=0, has_side_effects=True, vmem_limit_bytes=63 * 1024 * 1024
        ),
        cost_estimate=pl.CostEstimate(flops=1_500_000_000, bytes_accessed=4_000_000, transcendentals=70_000),
    )(*args)


def solution(mesh):
    tokens = P("section", "expert", None)
    saved = P("section", None, None, "expert")
    cols = P("section", None, "expert")
    in_specs = (tokens,) * 8 + (saved, saved, cols, cols, tokens)
    return jax.shard_map(local, mesh=mesh, in_specs=in_specs, out_specs=(tokens, tokens), check_vma=False)
```
